32 devices in a mesh: grp: 2 (over x), ep: 16 (over z, y, core).
Axes of the slice: x: 2, y: 2, z: 4, core: 2. Of those that a mesh axis runs over, the one named last changes fastest.
Arguments:
- tokens_one: bfloat16 [1024, 2048], P(('grp', 'ep')), may hold values from -6 to 6
- routes_one: int32 [1024, 6], P(('grp', 'ep')), may hold values from 0 to 15, all different within a row; in each aligned block of 32 rows (0 to 31, 32 to 63, ...) at most 18 rows name the same one
- gates_one: bfloat16 [1024, 6], P(('grp', 'ep')), may hold values from 0.049804688 to 0.3984375
- tokens_two: bfloat16 [1024, 2048], P(('grp', 'ep')), may hold values from -6 to 6
- routes_two: int32 [1024, 6], P(('grp', 'ep')), may hold values from 0 to 15, all different within a row; in each aligned block of 32 rows (0 to 31, 32 to 63, ...) at most 18 rows name the same one
- gates_two: bfloat16 [1024, 6], P(('grp', 'ep')), may hold values from 0.049804688 to 0.3984375
- old_table: int32 [16], replicated, may hold values from 0 to 15, each once
- new_table: int32 [16], replicated, may hold values from 0 to 15, each once
- gate_up: bfloat16 [16, 2048, 1408], P('ep'), may hold values from -0.125 to 0.125
- down_proj: bfloat16 [16, 704, 2048], P('ep'), may hold values from -0.21875 to 0.21875
- norm_gain: bfloat16 [2048], replicated, may hold values from 0.099609375 to 1.8984375
- kv_weight: bfloat16 [2048, 1024], P(None, 'grp'), may hold values from -0.125 to 0.125
Outputs:
- hidden_one: bfloat16 [1024, 2048], P(('grp', 'ep'))
- kv_one: bfloat16 [1024, 1024], P(('grp', 'ep'))
- hidden_two: bfloat16 [1024, 2048], P(('grp', 'ep'))
- kv_two: bfloat16 [1024, 1024], P(('grp', 'ep'))
- gate_up_new: bfloat16 [16, 2048, 1408], P('ep', 'grp')
- down_proj_new: bfloat16 [16, 704, 2048], P('ep', None, 'grp')
The draws below stay inside these ranges and needn't reach their ends.
Inputs may be any that keep to these rules, and one draw needn't show every extreme that they name: `routes_one`: each row names 6 different slots; among the rows of one device no slot is named by more than 18 routes, a bound that some block reaches. `routes_two`: each row names 6 different slots; among the rows of one device no slot is named by more than 18 routes, a bound that some block reaches. `old_table`: each expert appears once. `new_table`: each expert appears once.
All inputs are finite; a program needn't handle non-finite values.
Results may differ from the reference program's by a relative error of at most 0.006.
Values may be sent and summed in bfloat16 or wider, within the bound.
No kernel may reach another device: no remote copies, remote signals or barrier semaphores. Data moves between devices by JAX's collectives and lax.ppermute only.
A program may use at most 128 MiB of HBM per device.

```python
import math
import jax
import jax.numpy as jnp
import numpy as np
from jax import lax

D = 2048
FFE = 704
TOP = 6
TOK_DEV = 32
EXPERTS = 16
CAP = 18
KVW = 1024
TOKENS = 1024
N_GRP = 2
N_EP = 16


def block_scale(stream_key, extent, shards, smallest, top_value):
    def one(dim, blocks):
        steps = jax.random.uniform(jax.random.fold_in(jax.random.fold_in(stream_key, 6), dim), (blocks,), jnp.float32, smallest / len(shards), top_value / len(shards))
        return jnp.repeat(jnp.exp(steps), extent[dim] // blocks).reshape((-1,) + (1,) * (len(extent) - dim - 1))

    gain = one(*shards[0])
    for cut in shards[1:]:
        gain = gain * one(*cut)
    return gain


def shared_out(own_key, own, number, rows, count, top, most, lean):
    order = jax.random.permutation(own_key, count)
    packed, ordinary = portions_of(count, rows * top, most, lean, True), portions_of(count, rows * top, most, lean, False)
    places = jnp.arange(count)

    def named(sizes, offset_by):
        used = int((sizes > 0).sum())
        fixed = max(1, used // 4)
        shifted = fixed + (places - fixed + offset_by * (used - fixed)) % max(1, count - fixed)
        return jnp.zeros((count,), jnp.int32).at[order[jnp.where(places < fixed, places, shifted)]].set(jnp.asarray(sizes, jnp.int32))

    sizes = jnp.where(number % 4 == 0, named(packed, number // 4), named(ordinary, number - number // 4 - 1))
    mixed = jax.random.permutation(jax.random.fold_in(own, 3), count)
    donor, taker = mixed[0:count // 2 * 2:2], mixed[1:count // 2 * 2:2]
    room = jnp.minimum(sizes[donor] - 1, most - sizes[taker]) // 2
    room = jnp.where((donor == order[0]) | (taker == order[0]) | (sizes[taker] == 0), 0, jnp.maximum(room, 0))
    shifted = jax.random.randint(jax.random.fold_in(own, 4), (count // 2,), 0, 1 << 20) % (room + 1)
    sizes = sizes.at[donor].add(-shifted).at[taker].add(shifted)
    members = jnp.searchsorted(jnp.cumsum(sizes), jnp.arange(rows * top), side="right").astype(jnp.int32)
    grid = members.reshape(top, rows).T
    grid = grid[jax.random.permutation(jax.random.fold_in(own, 1), rows)]
    offset_by = jax.random.randint(jax.random.fold_in(own, 2), (rows, 1), 0, top)
    return jnp.take_along_axis(grid, (jnp.arange(top)[None, :] + offset_by) % top, axis=1)


def portions_of(amount, total, reach, slope, full):
    portions = [(1 << 20) // math.isqrt(rank ** slope) + 1 for rank in range(1, amount + 1)]
    largest = reach if full else min(reach, max(-(-total // amount), total * portions[0] // sum(portions)))
    least = 1 if total - largest >= amount - 1 else 0
    holding, surplus = [largest] + [least] * (amount - 1), total - largest - least * (amount - 1)
    while surplus > 0:
        candidates = [i for i in range(1, amount) if holding[i] < largest] or [i for i in range(1, amount) if holding[i] < reach]
        mass, budget = sum([portions[i] for i in candidates]), surplus
        for i in candidates:
            addition = min(reach - holding[i], max(1, budget * portions[i] // mass), surplus)
            holding[i] = holding[i] + addition
            surplus = surplus - addition
    return np.array(holding)


def normal_values(own_key, dims, width, most, shards=(), kind=jnp.bfloat16):
    loudness = block_scale(own_key, dims, shards, -0.22, 0.18) if shards else 1.0
    values = jax.random.normal(own_key, dims, jnp.float32) * width * loudness
    return jnp.minimum(jnp.maximum(values, -most), most).astype(kind)


def setup_inputs(seed: int = 0) -> dict:
    seeds = jax.random.split(jax.random.key(seed), 13)
    tokens_one = normal_values(seeds[0], (TOKENS, D), 1.0, 6.0, ((0, 32),))
    routes_one_keys = jax.random.split(jax.random.fold_in(seeds[1], 1), TOKENS // TOK_DEV)
    routes_one_turns = jax.random.permutation(jax.random.fold_in(seeds[1], 3), TOKENS // TOK_DEV)
    routes_one = jax.vmap(lambda own, number: shared_out(jax.random.fold_in(seeds[1], 2), own, number, TOK_DEV, EXPERTS, TOP, CAP, 2))(routes_one_keys, routes_one_turns).reshape((TOKENS, TOP))
    gates_one = jnp.clip(0.049804688 + 0.3486328 * jax.random.uniform(seeds[2], (TOKENS, TOP), jnp.float32) ** block_scale(seeds[2], (TOKENS, TOP), ((0, 32),), -0.2, 0.2), 0.049804688, 0.3984375).astype(jnp.bfloat16)
    tokens_two = normal_values(seeds[3], (TOKENS, D), 1.0, 6.0, ((0, 32),))
    routes_two_keys = jax.random.split(jax.random.fold_in(seeds[4], 1), TOKENS // TOK_DEV)
    routes_two_turns = jax.random.permutation(jax.random.fold_in(seeds[4], 3), TOKENS // TOK_DEV)
    routes_two = jax.vmap(lambda own, number: shared_out(jax.random.fold_in(seeds[4], 2), own, number, TOK_DEV, EXPERTS, TOP, CAP, 2))(routes_two_keys, routes_two_turns).reshape((TOKENS, TOP))
    gates_two = jnp.clip(0.049804688 + 0.3486328 * jax.random.uniform(seeds[5], (TOKENS, TOP), jnp.float32) ** block_scale(seeds[5], (TOKENS, TOP), ((0, 32),), -0.2, 0.2), 0.049804688, 0.3984375).astype(jnp.bfloat16)
    old_table = jax.random.permutation(seeds[6], EXPERTS).astype(jnp.int32)
    new_table = jax.random.permutation(seeds[7], EXPERTS).astype(jnp.int32)
    gate_up = normal_values(seeds[8], (EXPERTS, D, 2 * FFE), D ** -0.5, 0.125, ((0, 16),))
    down_proj = normal_values(seeds[9], (EXPERTS, FFE, D), FFE ** -0.5, 0.21875, ((0, 16),))
    norm_gain = jnp.clip(1.0 + 0.18 * jax.random.normal(seeds[10], (D,), jnp.float32), 0.099609375, 1.8984375).astype(jnp.bfloat16)
    kv_weight = normal_values(seeds[11], (D, KVW), D ** -0.5, 0.125, ((1, 2),))
    return dict(tokens_one=tokens_one, routes_one=routes_one, gates_one=gates_one, tokens_two=tokens_two, routes_two=routes_two, gates_two=gates_two, old_table=old_table, new_table=new_table, gate_up=gate_up, down_proj=down_proj, norm_gain=norm_gain, kv_weight=kv_weight)


def expert_ffn(activation, weight_in, weight_out):
    joined = jnp.dot(activation, weight_in, preferred_element_type=jnp.float32)
    gate_part = joined[:, :FFE]
    upward = joined[:, FFE:]
    hidden = (jax.nn.silu(gate_part) * upward).astype(jnp.bfloat16)
    return jnp.dot(hidden, weight_out, preferred_element_type=jnp.float32).astype(jnp.bfloat16)

def routed_layer(tokens, owners, gate_share, gate_up, down_proj):
    flattened = owners.reshape(-1).astype(jnp.int32)
    entries = flattened.shape[0]
    ordering = jnp.argsort(flattened, stable=True).astype(jnp.int32)
    numbers = jnp.arange(EXPERTS, dtype=jnp.int32)
    counts = lax.optimization_barrier(jnp.sum((flattened[:, None] == numbers[None, :]).astype(jnp.int32), axis=0))
    starts = (jnp.cumsum(counts) - counts).astype(jnp.int32)
    longest = N_GRP * N_EP * CAP
    padded = jnp.concatenate([ordering, jnp.full((longest,), entries, jnp.int32)])

    def visit_one(collected, expert):
        chosen = lax.dynamic_slice(padded, (starts[expert],), (longest,))
        chosen = jnp.where(jnp.arange(longest, dtype=jnp.int32) < counts[expert], chosen, entries)
        activation = tokens[jnp.minimum(chosen, entries - 1) // TOP]
        result = expert_ffn(activation, gate_up[expert], down_proj[expert])
        return (collected.at[chosen].set(result), None)
    collected = lax.scan(visit_one, jnp.zeros((entries + 1, D), jnp.bfloat16), numbers)[0]
    outputs = collected[:entries].reshape(tokens.shape[0], TOP, D).astype(jnp.float32)
    mixture = jnp.einsum('tk,tkd->td', gate_share.astype(jnp.float32), outputs)
    return (tokens.astype(jnp.float32) + mixture).astype(jnp.bfloat16)

def rms_norm(hidden, norm_gain):
    values = hidden.astype(jnp.float32)
    inverse_rms = lax.rsqrt(lax.optimization_barrier(jnp.mean(values * values, axis=-1, keepdims=True)) + 1e-06)
    return (values * inverse_rms * norm_gain.astype(jnp.float32)).astype(jnp.bfloat16)

def reference(tokens_one, routes_one, gates_one, tokens_two, routes_two, gates_two, old_table, new_table, gate_up, down_proj, norm_gain, kv_weight):
    old_inverse = jnp.zeros((EXPERTS,), jnp.int32).at[old_table].set(jnp.arange(EXPERTS, dtype=jnp.int32))
    sources_new = old_inverse[new_table].astype(jnp.int32)
    gate_up_new = gate_up[sources_new]
    down_proj_new = down_proj[sources_new]
    hidden_one = routed_layer(tokens_one, routes_one, gates_one, gate_up, down_proj)
    hidden_two = routed_layer(tokens_two, routes_two, gates_two, gate_up_new, down_proj_new)
    kv_one = jnp.dot(rms_norm(hidden_one, norm_gain), kv_weight, preferred_element_type=jnp.float32).astype(jnp.bfloat16)
    kv_two = jnp.dot(rms_norm(hidden_two, norm_gain), kv_weight, preferred_element_type=jnp.float32).astype(jnp.bfloat16)
    return (hidden_one, kv_one, hidden_two, kv_two, gate_up_new, down_proj_new)
```

```python
import jax
import jax.numpy as jnp
from jax import lax
from jax.sharding import PartitionSpec as P

TOP = 6
LANES = 128
BF = jnp.bfloat16
F32 = jnp.float32


def rms_norm(hidden, norm_gain):
    values = hidden.astype(F32)
    inverse_rms = lax.rsqrt(jnp.mean(values * values, axis=-1, keepdims=True) + 1e-06)
    return (values * inverse_rms * norm_gain.astype(F32)).astype(BF)


def local(
    tokens_one,
    routes_one,
    gates_one,
    tokens_two,
    routes_two,
    gates_two,
    old_table,
    new_table,
    gate_up,
    down_proj,
    norm_gain,
    kv_weight,
):
    w_in = gate_up[0]
    w_out = down_proj[0]
    ep = lax.axis_size("ep")
    grp = lax.axis_size("grp")
    me = lax.axis_index("ep")
    gi = lax.axis_index("grp")
    rows = tokens_one.shape[0]
    feat = w_in.shape[0]
    inner = w_out.shape[0]
    numbers = jnp.arange(ep, dtype=jnp.int32)
    sources_new = jnp.sum(
        (new_table[:, None] == old_table[None, :]).astype(jnp.int32) * numbers[None, :], axis=1
    )
    new_here = jnp.sum((sources_new == me).astype(jnp.int32) * numbers)

    part_rows = feat // grp
    half_in = lax.dynamic_slice_in_dim(w_in, gi * part_rows, part_rows, 0)
    half_out = lax.dynamic_slice_in_dim(w_out, gi * part_rows, part_rows, 1)
    half_in = half_in.reshape(ep, part_rows // ep, 2 * inner)
    nr = 8
    nc = ep // nr
    half_out = (
        half_out.reshape(nr, inner // nr, nc, part_rows // nc)
        .transpose(0, 2, 1, 3)
        .reshape(ep, inner // nr, part_rows // nc)
    )

    def a2a(x):
        return lax.all_to_all(x, "ep", split_axis=0, concat_axis=0, tiled=True)

    def ext(tok, gat, rou):
        pad = jnp.zeros((rows, LANES - 2 * TOP), BF)
        return jnp.concatenate([tok, gat, rou.astype(BF), pad], axis=1)

    mine = jnp.concatenate(
        [ext(tokens_one, gates_one, routes_one), ext(tokens_two, gates_two, routes_two)], axis=0
    )
    everyone = lax.all_gather(mine, "ep", axis=0, tiled=True)
    act = everyone[:, :feat]
    gat = everyone[:, feat : feat + TOP].astype(F32).reshape(ep, 2, rows, TOP)
    rou = everyone[:, feat + TOP : feat + 2 * TOP].astype(jnp.int32).reshape(ep, 2, rows, TOP)
    target = jnp.stack([me, new_here])[None, :, None, None]
    share = jnp.sum(jnp.where(rou == target, gat, 0.0), axis=-1).reshape(ep * 2 * rows, 1)

    joined = jnp.dot(act, w_in, preferred_element_type=F32)
    hidden = (jax.nn.silu(joined[:, :inner]) * joined[:, inner:]).astype(BF)
    out = jnp.dot(hidden, w_out, preferred_element_type=F32)
    partial = (out * share).astype(BF)
    mix = lax.psum_scatter(partial, "ep", scatter_dimension=0, tiled=True)

    spread_in = a2a(half_in)
    spread_out = a2a(half_out)
    new_in = a2a(spread_in[sources_new])
    new_out = a2a(spread_out[sources_new])
    gate_up_new = new_in.reshape(1, part_rows, 2 * inner)
    down_proj_new = (
        new_out.reshape(nr, nc, inner // nr, part_rows // nc)
        .transpose(0, 2, 1, 3)
        .reshape(1, inner, part_rows)
    )

    own = jnp.concatenate([tokens_one, tokens_two], axis=0)
    hidden_all = (own.astype(F32) + mix.astype(F32)).astype(BF)
    normed = rms_norm(hidden_all, norm_gain)
    kv = jnp.dot(
        normed,
        lax.all_gather(kv_weight, "grp", axis=1, tiled=True),
        preferred_element_type=F32,
    ).astype(BF)
    return (
        hidden_all[:rows],
        kv[:rows],
        hidden_all[rows:],
        kv[rows:],
        gate_up_new,
        down_proj_new,
    )


def solution(mesh):
    tok = P(("grp", "ep"), None)
    return jax.shard_map(
        local,
        mesh=mesh,
        in_specs=(
            tok,
            tok,
            tok,
            tok,
            tok,
            tok,
            P(),
            P(),
            P("ep", None, None),
            P("ep", None, None),
            P(),
            P(None, "grp"),
        ),
        out_specs=(tok, tok, tok, tok, P("ep", "grp", None), P("ep", None, "grp")),
        check_vma=False,
    )
```

```python
import jax
import jax.numpy as jnp
from jax import lax
from jax.sharding import PartitionSpec as P

TOP = 6
LANES = 128
BF = jnp.bfloat16
F32 = jnp.float32


def rms_norm(hidden, norm_gain):
    values = hidden.astype(F32)
    inverse_rms = lax.rsqrt(jnp.mean(values * values, axis=-1, keepdims=True) + 1e-06)
    return (values * inverse_rms * norm_gain.astype(F32)).astype(BF)


def swap(x, axis, distance):
    size = lax.axis_size(axis)
    return lax.ppermute(x, axis, [(i, i ^ distance) for i in range(size)])


def gather_bits(x, axis, bits):
    for bit in bits:
        x = jnp.concatenate([x, swap(x, axis, 1 << bit)], axis=0)
    return x


def reduce_bits(x, axis, bits):
    for bit in bits:
        half = x.shape[0] // 2
        x = x[:half] + swap(x[half:].astype(BF), axis, 1 << bit).astype(F32)
    return x


def experts(rows, target, w_in, w_out, feat):
    inner = w_out.shape[0]
    act = rows[:, :feat]
    gat = rows[:, feat : feat + TOP].astype(F32)
    rou = rows[:, feat + TOP : feat + 2 * TOP].astype(jnp.int32)
    share = jnp.sum(jnp.where(rou == target, gat, 0.0), axis=-1, keepdims=True)
    joined = jnp.dot(act, w_in, preferred_element_type=F32)
    hidden = (jax.nn.silu(joined[:, :inner]) * joined[:, inner:]).astype(BF)
    return jnp.dot(hidden, w_out, preferred_element_type=F32) * share


def local(
    tokens_one,
    routes_one,
    gates_one,
    tokens_two,
    routes_two,
    gates_two,
    old_table,
    new_table,
    gate_up,
    down_proj,
    norm_gain,
    kv_weight,
):
    ep = lax.axis_size("ep")
    grp = lax.axis_size("grp")
    half = ep // 2
    me = lax.axis_index("ep")
    gi = lax.axis_index("grp")
    me_low = me % half
    my_half = me // half
    rows = tokens_one.shape[0]
    feat = gate_up.shape[1]
    inner = down_proj.shape[1]
    part_rows = feat // grp
    bits = ep.bit_length() - 1
    grp_bits = grp.bit_length() - 1

    numbers = jnp.arange(ep, dtype=jnp.int32)
    sources = jnp.sum(
        (new_table[:, None] == old_table[None, :]).astype(jnp.int32) * numbers[None, :], axis=1
    )
    new_here = jnp.sum((sources == me).astype(jnp.int32) * numbers)
    crosses = (sources // half) != (numbers // half)
    to_here = numbers // half == my_half
    count = jnp.sum((crosses & (numbers < half)).astype(jnp.int32))
    rank_all = jnp.cumsum(crosses.astype(jnp.int32)) - crosses.astype(jnp.int32)
    rank = jnp.where(numbers < half, rank_all, rank_all - count)
    outgoing = crosses & ~to_here
    places = jnp.arange(half, dtype=jnp.int32)
    out_source = jnp.sum(
        jnp.where(
            outgoing[None, :] & (rank[None, :] == places[:, None]), (sources % half)[None, :], 0
        ),
        axis=1,
    )
    out_pick = out_source ^ me_low
    slot_source = jnp.where(crosses, half + rank, (sources % half) ^ me_low)
    slot_pick = slot_source[my_half * half + (me_low ^ places)]

    def branch(most):
        def run(_):
            kv_blocks = [kv_weight]
            for bit in range(grp_bits):
                kv_blocks = kv_blocks + [swap(x, "grp", 1 << bit) for x in kv_blocks]

            def ext(tok, gat, rou):
                pad = jnp.zeros((rows, LANES - 2 * TOP), BF)
                return jnp.concatenate([tok, gat, rou.astype(BF), pad], axis=1)

            high = list(range(bits - 1, 1, -1))
            orders = (high + [1, 0], [1] + high + [0])
            own = (tokens_one, tokens_two)
            given = (
                ext(tokens_one, gates_one, routes_one),
                ext(tokens_two, gates_two, routes_two),
            )
            mixed = []
            for x, order, target in zip(given, orders, (me, new_here)):
                everyone = gather_bits(x, "ep", order)
                partial = experts(everyone, target, gate_up[0], down_proj[0], feat)
                mixed.append(reduce_bits(partial, "ep", order[::-1]))
            hidden = [(t.astype(F32) + m).astype(BF) for t, m in zip(own, mixed)]

            def moved(piece):
                pooled = [piece(me_low ^ d) for d in range(half)]
                pooled = [pooled[0]] + [swap(pooled[d], "ep", d) for d in range(1, half)]
                pool = jnp.stack(pooled)
                sent = jnp.take(pool, out_pick[:most], axis=0)
                pool = jnp.concatenate([pool, swap(sent, "ep", half)], axis=0)
                back = [
                    lax.dynamic_index_in_dim(pool, slot_pick[d], 0, keepdims=False)
                    for d in range(half)
                ]
                back = [back[0]] + [swap(back[d], "ep", d) for d in range(1, half)]
                return jnp.take(jnp.stack(back), me_low ^ places, axis=0)

            cut = part_rows // 2 // half

            def gate_piece(chunk):
                return lambda p: lax.dynamic_slice(
                    gate_up[0],
                    (gi * part_rows + chunk * (part_rows // 2) + p * cut, 0),
                    (cut, 2 * inner),
                )

            down_cut = inner // half

            def down_piece(p):
                return lax.dynamic_slice(
                    down_proj[0], (p * down_cut, gi * part_rows), (down_cut, part_rows)
                )

            gate_up_new = jnp.concatenate(
                [moved(gate_piece(c)).reshape(part_rows // 2, 2 * inner) for c in range(2)], axis=0
            )[None]
            down_proj_new = moved(down_piece).reshape(1, inner, part_rows)

            normed = rms_norm(jnp.concatenate(hidden, axis=0), norm_gain)
            blocks = [jnp.dot(normed, w, preferred_element_type=F32).astype(BF) for w in kv_blocks]
            kv = jnp.take(jnp.stack(blocks), gi ^ jnp.arange(grp), axis=0)
            kv = kv.transpose(1, 0, 2).reshape(2 * rows, -1)
            return hidden[0], kv[:rows], hidden[1], kv[rows:], gate_up_new, down_proj_new

        return run

    steps = (-1, 0, 1, 2) if half <= 8 else (2,)
    sizes = sorted({min(half, max(1, half // 2 + i)) for i in steps} | {half})
    index = sum((count > s).astype(jnp.int32) for s in sizes[:-1])
    return lax.switch(index, [branch(s) for s in sizes], 0)


def solution(mesh):
    tok = P(("grp", "ep"), None)
    return jax.shard_map(
        local,
        mesh=mesh,
        in_specs=(
            tok,
            tok,
            tok,
            tok,
            tok,
            tok,
            P(),
            P(),
            P("ep", None, None),
            P("ep", None, None),
            P(),
            P(None, "grp"),
        ),
        out_specs=(tok, tok, tok, tok, P("ep", "grp", None), P("ep", None, "grp")),
        check_vma=False,
    )
```

```python
import jax
import jax.numpy as jnp
from jax import lax
from jax.sharding import PartitionSpec as P

TOP = 6
LANES = 128
BF = jnp.bfloat16
F32 = jnp.float32


def rms_norm(hidden, norm_gain):
    values = hidden.astype(F32)
    inverse_rms = lax.rsqrt(jnp.mean(values * values, axis=-1, keepdims=True) + 1e-06)
    return (values * inverse_rms * norm_gain.astype(F32)).astype(BF)


def swap(x, axis, distance):
    size = lax.axis_size(axis)
    return lax.ppermute(x, axis, [(i, i ^ distance) for i in range(size)])


def gather_bits(x, axis, bits):
    for bit in bits:
        x = jnp.concatenate([x, swap(x, axis, 1 << bit)], axis=0)
    return x


def reduce_bits(x, axis, bits):
    for bit in bits:
        half = x.shape[0] // 2
        x = x[:half] + swap(x[half:].astype(BF), axis, 1 << bit).astype(F32)
    return x


def experts(rows, target, w_in, w_out, feat):
    inner = w_out.shape[0]
    act = rows[:, :feat]
    gat = rows[:, feat : feat + TOP].astype(F32)
    rou = rows[:, feat + TOP : feat + 2 * TOP].astype(jnp.int32)
    share = jnp.sum(jnp.where(rou == target, gat, 0.0), axis=-1, keepdims=True)
    joined = jnp.dot(act, w_in, preferred_element_type=F32)
    hidden = (jax.nn.silu(joined[:, :inner]) * joined[:, inner:]).astype(BF)
    return jnp.dot(hidden, w_out, preferred_element_type=F32) * share


def local(
    tokens_one,
    routes_one,
    gates_one,
    tokens_two,
    routes_two,
    gates_two,
    old_table,
    new_table,
    gate_up,
    down_proj,
    norm_gain,
    kv_weight,
):
    ep = lax.axis_size("ep")
    grp = lax.axis_size("grp")
    me = lax.axis_index("ep")
    gi = lax.axis_index("grp")
    rows = tokens_one.shape[0]
    feat = gate_up.shape[1]
    inner = down_proj.shape[1]
    part_rows = feat // grp
    bits = ep.bit_length() - 1
    grp_bits = grp.bit_length() - 1

    numbers = jnp.arange(ep, dtype=jnp.int32)
    sources = jnp.sum(
        (new_table[:, None] == old_table[None, :]).astype(jnp.int32) * numbers[None, :], axis=1
    )
    new_here = jnp.sum((sources == me).astype(jnp.int32) * numbers)

    kv_blocks = [kv_weight]
    for bit in range(grp_bits):
        kv_blocks = kv_blocks + [swap(x, "grp", 1 << bit) for x in kv_blocks]

    def ext(tok, gat, rou):
        pad = jnp.zeros((rows, LANES - 2 * TOP), BF)
        return jnp.concatenate([tok, gat, rou.astype(BF), pad], axis=1)

    high = list(range(bits - 1, 1, -1))
    orders = (high + [1, 0], [1] + high + [0])
    own = (tokens_one, tokens_two)
    given = (
        ext(tokens_one, gates_one, routes_one),
        ext(tokens_two, gates_two, routes_two),
    )
    mixed = []
    for x, order, target in zip(given, orders, (me, new_here)):
        everyone = gather_bits(x, "ep", order)
        partial = experts(everyone, target, gate_up[0], down_proj[0], feat)
        mixed.append(reduce_bits(partial, "ep", order[::-1]))
    hidden = [(t.astype(F32) + m).astype(BF) for t, m in zip(own, mixed)]

    half_in = lax.dynamic_slice_in_dim(gate_up[0], gi * part_rows, part_rows, 0)
    half_out = lax.dynamic_slice_in_dim(down_proj[0], gi * part_rows, part_rows, 1)
    half_in = half_in.reshape(ep, part_rows // ep, 2 * inner)
    nr = 8
    nc = ep // nr
    half_out = (
        half_out.reshape(nr, inner // nr, nc, part_rows // nc)
        .transpose(0, 2, 1, 3)
        .reshape(ep, inner // nr, part_rows // nc)
    )

    def a2a(x):
        return lax.all_to_all(x, "ep", split_axis=0, concat_axis=0, tiled=True)

    spread_in = a2a(half_in)
    spread_out = a2a(half_out)
    new_in = a2a(spread_in[sources])
    new_out = a2a(spread_out[sources])
    gate_up_new = new_in.reshape(1, part_rows, 2 * inner)
    down_proj_new = (
        new_out.reshape(nr, nc, inner // nr, part_rows // nc)
        .transpose(0, 2, 1, 3)
        .reshape(1, inner, part_rows)
    )

    normed = rms_norm(jnp.concatenate(hidden, axis=0), norm_gain)
    blocks = [jnp.dot(normed, w, preferred_element_type=F32).astype(BF) for w in kv_blocks]
    kv = jnp.take(jnp.stack(blocks), gi ^ jnp.arange(grp), axis=0)
    kv = kv.transpose(1, 0, 2).reshape(2 * rows, -1)
    return hidden[0], kv[:rows], hidden[1], kv[rows:], gate_up_new, down_proj_new


def solution(mesh):
    tok = P(("grp", "ep"), None)
    return jax.shard_map(
        local,
        mesh=mesh,
        in_specs=(
            tok,
            tok,
            tok,
            tok,
            tok,
            tok,
            P(),
            P(),
            P("ep", None, None),
            P("ep", None, None),
            P(),
            P(None, "grp"),
        ),
        out_specs=(tok, tok, tok, tok, P("ep", "grp", None), P("ep", None, "grp")),
        check_vma=False,
    )
```

```python
import jax
import jax.numpy as jnp
from jax import lax
from jax.sharding import PartitionSpec as P

TOP = 6
LANES = 128
BF = jnp.bfloat16
F32 = jnp.float32


def rms_norm(hidden, norm_gain):
    values = hidden.astype(F32)
    inverse_rms = lax.rsqrt(jnp.mean(values * values, axis=-1, keepdims=True) + 1e-06)
    return (values * inverse_rms * norm_gain.astype(F32)).astype(BF)


def swap(x, axis, distance):
    size = lax.axis_size(axis)
    return lax.ppermute(x, axis, [(i, i ^ distance) for i in range(size)])


def experts(rows, target, w_in, w_out, feat):
    inner = w_out.shape[0]
    act = rows[:, :feat]
    gat = rows[:, feat : feat + TOP].astype(F32)
    rou = rows[:, feat + TOP : feat + 2 * TOP].astype(jnp.int32)
    share = jnp.sum(jnp.where(rou == target, gat, 0.0), axis=-1, keepdims=True)
    joined = jnp.dot(act, w_in, preferred_element_type=F32)
    hidden = (jax.nn.silu(joined[:, :inner]) * joined[:, inner:]).astype(BF)
    return jnp.dot(hidden, w_out, preferred_element_type=F32) * share


def local(
    tokens_one,
    routes_one,
    gates_one,
    tokens_two,
    routes_two,
    gates_two,
    old_table,
    new_table,
    gate_up,
    down_proj,
    norm_gain,
    kv_weight,
):
    ep = lax.axis_size("ep")
    grp = lax.axis_size("grp")
    chips = ep // 2
    me = lax.axis_index("ep")
    gi = lax.axis_index("grp")
    chip, core = me // 2, me % 2
    rows = tokens_one.shape[0]
    feat = gate_up.shape[1]
    inner = down_proj.shape[1]
    part_rows = feat // grp
    grp_bits = grp.bit_length() - 1

    numbers = jnp.arange(ep, dtype=jnp.int32)
    sources = jnp.sum(
        (new_table[:, None] == old_table[None, :]).astype(jnp.int32) * numbers[None, :], axis=1
    )
    new_here = jnp.sum((sources == me).astype(jnp.int32) * numbers)

    def ext(tok, gat, rou):
        pad = jnp.zeros((rows, LANES - 2 * TOP), BF)
        return jnp.concatenate([tok, gat, rou.astype(BF), pad], axis=1)

    mine = jnp.concatenate(
        [ext(tokens_one, gates_one, routes_one), ext(tokens_two, gates_two, routes_two)], axis=0
    )
    far = [4 * i for i in range(1, ep // 4)]
    here = jnp.concatenate([mine] + [swap(mine, "ep", d) for d in far], axis=0)
    here = jnp.concatenate([here, swap(here, "ep", 2)], axis=0)
    here, gi_gate = lax.optimization_barrier((here, gi))
    there = swap(here, "ep", 1)
    target = jnp.concatenate([jnp.full((rows, 1), me), jnp.full((rows, 1), new_here)], axis=0)
    target = jnp.tile(target, (ep // 2, 1))
    w_in, w_out = gate_up[0], down_proj[0]
    kept = experts(here, target, w_in, w_out, feat)
    given = experts(there, target, w_in, w_out, feat).astype(BF)

    kept = kept + swap(given, "ep", 1).astype(F32)
    half = kept.shape[0] // 2
    kept = kept[:half] + swap(kept[half:].astype(BF), "ep", 2).astype(F32)
    distance = jnp.arange(chips, dtype=jnp.int32)
    slot_source = sources[2 * (chip ^ distance) + core]
    from_mine = slot_source % 2 == core
    at = (slot_source // 2) ^ chip
    kept, at_gate = lax.optimization_barrier((kept, at))
    block = 2 * rows
    mix = kept[:block]
    for i, d in enumerate(far):
        mix = mix + swap(kept[(i + 1) * block : (i + 2) * block].astype(BF), "ep", d).astype(F32)
    own = jnp.concatenate([tokens_one, tokens_two], axis=0)
    hidden = (own.astype(F32) + mix).astype(BF)

    new_source = sources[me]

    def moved(piece, at):
        first = [piece(0)] + [swap(piece(d), "ep", 2 * d) for d in range(1, chips)]
        first = jnp.stack(first)
        other = swap(first, "ep", 1)
        second = [
            jnp.where(
                from_mine[d],
                lax.dynamic_index_in_dim(first, at[d], 0, keepdims=False),
                lax.dynamic_index_in_dim(other, at[d], 0, keepdims=False),
            )
            for d in range(chips)
        ]
        second = [second[0]] + [swap(second[d], "ep", 2 * d) for d in range(1, chips)]
        out = jnp.zeros((chips,) + first.shape[1:], BF)
        for d in range(chips):
            out = lax.dynamic_update_index_in_dim(
                out, second[d], chip ^ d ^ (new_source // 2), 0
            )
        return out

    gate_cut = part_rows // chips
    down_cut = inner // chips

    def gate_piece(d):
        start = gi_gate * part_rows + d * gate_cut
        return lax.dynamic_slice(w_in, (start, 0), (gate_cut, 2 * inner))

    def down_piece(d):
        return lax.dynamic_slice(w_out, (d * down_cut, gi * part_rows), (down_cut, part_rows))

    gate_up_new = moved(gate_piece, at_gate).reshape(1, part_rows, 2 * inner)
    down_proj_new = moved(down_piece, at).reshape(1, inner, part_rows)

    kv_blocks = [kv_weight]
    for bit in range(grp_bits):
        kv_blocks = kv_blocks + [swap(x, "grp", 1 << bit) for x in kv_blocks]
    normed = rms_norm(hidden, norm_gain)
    blocks = [jnp.dot(normed, w, preferred_element_type=F32).astype(BF) for w in kv_blocks]
    kv = jnp.take(jnp.stack(blocks), gi ^ jnp.arange(grp), axis=0)
    kv = kv.transpose(1, 0, 2).reshape(2 * rows, -1)
    return hidden[:rows], kv[:rows], hidden[rows:], kv[rows:], gate_up_new, down_proj_new


def solution(mesh):
    tok = P(("grp", "ep"), None)
    return jax.shard_map(
        local,
        mesh=mesh,
        in_specs=(
            tok,
            tok,
            tok,
            tok,
            tok,
            tok,
            P(),
            P(),
            P("ep", None, None),
            P("ep", None, None),
            P(),
            P(None, "grp"),
        ),
        out_specs=(tok, tok, tok, tok, P("ep", "grp", None), P("ep", None, "grp")),
        check_vma=False,
    )
```

```python
import jax
import jax.numpy as jnp
from jax import lax
from jax.experimental import pallas as pl
from jax.experimental.pallas import tpu as pltpu
from jax.sharding import PartitionSpec as P

TOP = 6
LANES = 128
BF = jnp.bfloat16
F32 = jnp.float32


def rms_norm(hidden, norm_gain):
    values = hidden.astype(F32)
    inverse_rms = lax.rsqrt(jnp.mean(values * values, axis=-1, keepdims=True) + 1e-06)
    return (values * inverse_rms * norm_gain.astype(F32)).astype(BF)


def swap(x, axis, distance):
    size = lax.axis_size(axis)
    return lax.ppermute(x, axis, [(i, i ^ distance) for i in range(size)])


def experts(rows, target, w_in, w_out, feat):
    inner = w_out.shape[0]
    act = rows[:, :feat]
    gat = rows[:, feat : feat + TOP].astype(F32)
    rou = rows[:, feat + TOP : feat + 2 * TOP].astype(jnp.int32)
    share = jnp.sum(jnp.where(rou == target, gat, 0.0), axis=-1, keepdims=True)
    joined = jnp.dot(act, w_in, preferred_element_type=F32)
    hidden = (jax.nn.silu(joined[:, :inner]) * joined[:, inner:]).astype(BF)
    return jnp.dot(hidden, w_out, preferred_element_type=F32) * share


def copies(jobs):
    for sources, pick, target, sem in jobs:
        if pick is None:
            pltpu.make_async_copy(sources[0], target, sem).start()
            continue
        for j, source in enumerate(sources):

            @pl.when(pick == j)
            def _():
                pltpu.make_async_copy(source, target, sem).start()

    for sources, _, target, sem in jobs:
        pltpu.make_async_copy(sources[0], target, sem).wait()


def block_call(body, name, index, operands, outs, count):
    any_spec = pl.BlockSpec(memory_space=pl.ANY)
    size = sum(o.size * 4 for o in outs)
    return pl.pallas_call(
        body,
        name=name,
        out_shape=outs,
        in_specs=[pl.BlockSpec(memory_space=pltpu.SMEM)] + [any_spec] * len(operands),
        out_specs=[any_spec] * len(outs),
        scratch_shapes=[pltpu.SemaphoreType.DMA((count,))],
        cost_estimate=pl.CostEstimate(flops=0, bytes_accessed=size, transcendentals=0),
    )(index, *operands)


def pool_of(refs, chips):
    kept, other = refs[:chips], refs[chips]
    return [other.at[j // 2] if j % 2 else kept[j // 2].at[0] for j in range(2 * chips)]


def pick_out(index, kept, other, most):
    chips = len(kept)

    def body(*refs):
        picks, out, sem = refs[0], refs[-2], refs[-1]
        pool = pool_of(refs[1:-2], chips)
        copies([(pool, picks[i], out.at[i], sem.at[i]) for i in range(most)])

    unit = other.shape[1:]
    return block_call(
        body, "pick_out", index, [*kept, other], [jax.ShapeDtypeStruct((most,) + unit, BF)], most
    )[0]


def pick_back(index, kept, other, came):
    chips = len(kept)
    most = came.shape[0]

    def body(*refs):
        picks, even, odd, sem = refs[0], refs[-3], refs[-2], refs[-1]
        pool = pool_of(refs[1 : 2 + chips], chips) + [refs[2 + chips].at[i] for i in range(most)]
        copies(
            [
                (pool, picks[2 * chips + t], (odd if t % 2 else even).at[t // 2], sem.at[t])
                for t in range(2 * chips)
            ]
        )

    out = jax.ShapeDtypeStruct((chips,) + other.shape[1:], BF)
    return block_call(body, "pick_back", index, [*kept, other, came], [out, out], 2 * chips)


def place(index, groups):
    chips = len(groups[0])
    units = 2 * chips
    flat = [x for group in groups for x in group]

    def body(*refs):
        picks, out, sem = refs[0], refs[-2], refs[-1]
        jobs = []
        for g in range(len(groups)):
            for t in range(units):
                source = refs[1 + g * chips + t // 2].at[t % 2]
                to = out.at[g * units + picks[2 * units + t]]
                jobs.append(([source], None, to, sem.at[g * units + t]))
        copies(jobs)

    total = len(groups) * units
    out = jax.ShapeDtypeStruct((total,) + groups[0][0].shape[1:], BF)
    return block_call(body, "place", index, flat, [out], total)[0]


def local(
    tokens_one,
    routes_one,
    gates_one,
    tokens_two,
    routes_two,
    gates_two,
    old_table,
    new_table,
    gate_up,
    down_proj,
    norm_gain,
    kv_weight,
):
    ep = lax.axis_size("ep")
    grp = lax.axis_size("grp")
    half = ep // 2
    chips = half // 2
    me = lax.axis_index("ep")
    gi = lax.axis_index("grp")
    rows = tokens_one.shape[0]
    feat = gate_up.shape[1]
    inner = down_proj.shape[1]
    part_rows = feat // grp
    grp_bits = grp.bit_length() - 1
    w_in, w_out = gate_up[0], down_proj[0]

    def ext(tok, gat, rou):
        pad = jnp.zeros((rows, LANES - 2 * TOP), BF)
        return jnp.concatenate([tok, gat, rou.astype(BF), pad], axis=1)

    mine = jnp.concatenate(
        [ext(tokens_one, gates_one, routes_one), ext(tokens_two, gates_two, routes_two)], axis=0
    )
    far = [4 * i for i in range(1, ep // 4)]
    line = jnp.concatenate([mine] + [swap(mine, "ep", d) for d in far], axis=0)

    gate_unit = part_rows // 2 // half
    down_unit = inner // half

    def gate_block(chunk, gi):
        def block(b):
            start = gi * part_rows + (chunk * half + 2 * b) * gate_unit
            piece = lax.dynamic_slice(w_in, (start, 0), (2 * gate_unit, 2 * inner))
            return piece.reshape(2, gate_unit, 2 * inner)

        return block

    def down_block(gi):
        def block(b):
            start = (2 * b * down_unit, gi * part_rows)
            piece = lax.dynamic_slice(w_out, start, (2 * down_unit, part_rows))
            return piece.reshape(2, down_unit, part_rows)

        return block

    def spread(block):
        kept = [block(0)] + [swap(block(b), "ep", 2 * b) for b in range(1, chips)]
        other = swap(jnp.concatenate([x[1:] for x in kept], axis=0), "ep", 1)
        return kept, other

    first = spread(gate_block(0, gi))

    numbers = jnp.arange(ep, dtype=jnp.int32)
    places = jnp.arange(half, dtype=jnp.int32)
    sources = jnp.sum(
        (new_table[:, None] == old_table[None, :]).astype(jnp.int32) * numbers[None, :], axis=1
    )
    new_here = jnp.sum((sources == me).astype(jnp.int32) * numbers)
    low = me % half
    crosses = (sources ^ numbers) >= half
    count = jnp.sum((crosses & (numbers < half)).astype(jnp.int32))
    before = (numbers[None, :] < numbers[:, None]) & ((numbers[None, :] ^ numbers[:, None]) < half)
    rank = jnp.sum((before & crosses[None, :]).astype(jnp.int32), axis=1)
    held = (sources % half) ^ low
    outgoing = crosses & ((numbers ^ me) >= half)
    out_pick = jnp.sum(
        jnp.where(outgoing[None, :] & (rank[None, :] == places[:, None]), held[None, :], 0), axis=1
    )
    code = jnp.where(crosses, half + rank, held)
    at_distance = numbers[None, :] == (places[:, None] ^ me)
    back_pick = jnp.sum(jnp.where(at_distance, code[None, :], 0), axis=1)
    own_held = jnp.sum(jnp.where(numbers == me, held, 0))
    index = jnp.concatenate([out_pick, back_pick, places ^ own_held])

    target = jnp.concatenate([jnp.full((rows, 1), me), jnp.full((rows, 1), new_here)], axis=0)
    target = jnp.tile(target, (ep // 2, 1))
    own = jnp.concatenate([tokens_one, tokens_two], axis=0)

    def collect(chunk, came):
        even, odd = pick_back(index, *chunk, came)
        odd = swap(odd, "ep", 1)
        sent = [jnp.concatenate([even[b : b + 1], odd[b : b + 1]], axis=0) for b in range(chips)]
        return [sent[0]] + [swap(sent[b], "ep", 2 * b) for b in range(1, chips)]

    def branch(most):
        def run(line, first):
            sent = pick_out(index, *first, most)
            came = [swap(sent, "ep", half)]
            later, _ = lax.optimization_barrier((gi, sent))

            here = jnp.concatenate([line, swap(line, "ep", 2)], axis=0)
            there = swap(here, "ep", 1)
            kept = experts(here, target, w_in, w_out, feat)
            given = experts(there, target, w_in, w_out, feat).astype(BF)

            chunks = [first, spread(gate_block(1, later)), spread(down_block(later))]
            for chunk in chunks[1:]:
                sent = pick_out(index, *chunk, most)
                came[-1], _ = lax.optimization_barrier((came[-1], sent))
                came.append(swap(sent, "ep", half))
            back = [collect(chunk, x) for chunk, x in zip(chunks, came)]
            gate_up_new = place(index, back[:2]).reshape(1, part_rows, 2 * inner)
            down_proj_new = place(index, back[2:]).reshape(1, inner, part_rows)

            kept = kept + swap(given, "ep", 1).astype(F32)
            middle = kept.shape[0] // 2
            kept = kept[:middle] + swap(kept[middle:].astype(BF), "ep", 2).astype(F32)
            block = 2 * rows
            mix = kept[:block]
            for i, d in enumerate(far):
                part = kept[(i + 1) * block : (i + 2) * block].astype(BF)
                mix = mix + swap(part, "ep", d).astype(F32)
            hidden = (own.astype(F32) + mix).astype(BF)

            kv_blocks = [lax.optimization_barrier((kv_weight, here))[0]]
            for bit in range(grp_bits):
                kv_blocks = kv_blocks + [swap(x, "grp", 1 << bit) for x in kv_blocks]
            normed = rms_norm(hidden, norm_gain)
            blocks = [jnp.dot(normed, w, preferred_element_type=F32).astype(BF) for w in kv_blocks]
            kv = jnp.take(jnp.stack(blocks), gi ^ jnp.arange(grp), axis=0)
            kv = kv.transpose(1, 0, 2).reshape(2 * rows, -1)
            return hidden[:rows], kv[:rows], hidden[rows:], kv[rows:], gate_up_new, down_proj_new

        return run

    steps = (-1, 0, 1, 2) if half <= 8 else (2,)
    sizes = sorted({min(half, max(1, half // 2 + i)) for i in steps} | {half})
    which = sum((count > s).astype(jnp.int32) for s in sizes[:-1])
    return lax.switch(which, [branch(s) for s in sizes], line, first)


def solution(mesh):
    tok = P(("grp", "ep"), None)
    return jax.shard_map(
        local,
        mesh=mesh,
        in_specs=(
            tok,
            tok,
            tok,
            tok,
            tok,
            tok,
            P(),
            P(),
            P("ep", None, None),
            P("ep", None, None),
            P(),
            P(None, "grp"),
        ),
        out_specs=(tok, tok, tok, tok, P("ep", "grp", None), P("ep", None, "grp")),
        check_vma=False,
    )
```

```python
import jax
import jax.numpy as jnp
from jax import lax
from jax.experimental import pallas as pl
from jax.experimental.pallas import tpu as pltpu
from jax.sharding import PartitionSpec as P

TOP = 6
LANES = 128
BF = jnp.bfloat16
F32 = jnp.float32


def rms_norm(hidden, norm_gain):
    values = hidden.astype(F32)
    inverse_rms = lax.rsqrt(jnp.mean(values * values, axis=-1, keepdims=True) + 1e-06)
    return (values * inverse_rms * norm_gain.astype(F32)).astype(BF)


def swap(x, axis, distance):
    size = lax.axis_size(axis)
    return lax.ppermute(x, axis, [(i, i ^ distance) for i in range(size)])


def a2a(x):
    return lax.all_to_all(x, "ep", split_axis=0, concat_axis=0, tiled=True)


def tiles(piece, pieces, unit, inner, columns):
    per_column = inner // unit
    for j in range(2 * inner // LANES):
        u = j * pieces + piece
        row = pl.multiple_of((u % per_column) * unit, unit)
        column = pl.multiple_of((u // per_column) * LANES, LANES)
        yield row, column, j * LANES


def pack(w_in, w_out, gi, part_rows, pieces):
    inner = w_out.shape[0]
    cut = part_rows // pieces
    unit = cut // 2
    step = 4

    def body(_, gate_ref, down_ref, out_ref):
        at = pl.program_id(0) * step
        for i in range(step):
            out_ref[i, :cut, :] = gate_ref[i * cut : (i + 1) * cut, :]
            for row, column, to in tiles(at + i, pieces, unit, inner, part_rows):
                out_ref[i, cut:, to : to + LANES] = down_ref[pl.ds(row, unit), pl.ds(column, LANES)]

    return pl.pallas_call(
        body,
        name="pack",
        out_shape=jax.ShapeDtypeStruct((pieces, cut + unit, 2 * inner), BF),
        grid_spec=pltpu.PrefetchScalarGridSpec(
            num_scalar_prefetch=1,
            grid=(pieces // step,),
            in_specs=[
                pl.BlockSpec((step * cut, 2 * inner), lambda p, g: (g[0] * (pieces // step) + p, 0)),
                pl.BlockSpec((inner, part_rows), lambda p, g: (0, g[0])),
            ],
            out_specs=pl.BlockSpec((step, cut + unit, 2 * inner), lambda p, g: (p, 0, 0)),
        ),
        compiler_params=pltpu.CompilerParams(vmem_limit_bytes=32 * 1024 * 1024),
        cost_estimate=pl.CostEstimate(
            flops=0, bytes_accessed=12 * part_rows * inner, transcendentals=0
        ),
    )(gi.reshape(1), w_in, w_out)


def unpack(packed, part_rows, inner):
    pieces = packed.shape[0]
    cut = part_rows // pieces
    unit = cut // 2
    step = 4

    def body(in_ref, gate_ref, down_ref):
        at = pl.program_id(0) * step
        for i in range(step):
            gate_ref[i * cut : (i + 1) * cut, :] = in_ref[i, :cut, :]
            for row, column, to in tiles(at + i, pieces, unit, inner, part_rows):
                down_ref[pl.ds(row, unit), pl.ds(column, LANES)] = in_ref[i, cut:, to : to + LANES]

    return pl.pallas_call(
        body,
        name="unpack",
        out_shape=[
            jax.ShapeDtypeStruct((part_rows, 2 * inner), BF),
            jax.ShapeDtypeStruct((inner, part_rows), BF),
        ],
        grid=(pieces // step,),
        in_specs=[pl.BlockSpec((step, cut + unit, 2 * inner), lambda p: (p, 0, 0))],
        out_specs=[
            pl.BlockSpec((step * cut, 2 * inner), lambda p: (p, 0)),
            pl.BlockSpec((inner, part_rows), lambda p: (0, 0)),
        ],
        compiler_params=pltpu.CompilerParams(vmem_limit_bytes=32 * 1024 * 1024),
        cost_estimate=pl.CostEstimate(
            flops=0, bytes_accessed=12 * part_rows * inner, transcendentals=0
        ),
    )(packed)


def local(
    tokens_one,
    routes_one,
    gates_one,
    tokens_two,
    routes_two,
    gates_two,
    old_table,
    new_table,
    gate_up,
    down_proj,
    norm_gain,
    kv_weight,
):
    w_in = gate_up[0]
    w_out = down_proj[0]
    ep = lax.axis_size("ep")
    grp = lax.axis_size("grp")
    me = lax.axis_index("ep")
    gi = lax.axis_index("grp")
    rows = tokens_one.shape[0]
    feat = w_in.shape[0]
    inner = w_out.shape[0]
    numbers = jnp.arange(ep, dtype=jnp.int32)
    sources_new = jnp.sum(
        (new_table[:, None] == old_table[None, :]).astype(jnp.int32) * numbers[None, :], axis=1
    )
    new_here = jnp.sum((sources_new == me).astype(jnp.int32) * numbers)

    kv_blocks = [kv_weight]
    for bit in range(grp.bit_length() - 1):
        kv_blocks = kv_blocks + [swap(x, "grp", 1 << bit) for x in kv_blocks]

    def ext(tok, gat, rou):
        pad = jnp.zeros((rows, LANES - 2 * TOP), BF)
        return jnp.concatenate([tok, gat, rou.astype(BF), pad], axis=1)

    mine = jnp.concatenate(
        [ext(tokens_one, gates_one, routes_one), ext(tokens_two, gates_two, routes_two)], axis=0
    )
    everyone = lax.all_gather(mine, "ep", axis=0, tiled=True)
    act = everyone[:, :feat]
    gat = everyone[:, feat : feat + TOP].astype(F32).reshape(ep, 2, rows, TOP)
    rou = everyone[:, feat + TOP : feat + 2 * TOP].astype(jnp.int32).reshape(ep, 2, rows, TOP)
    target = jnp.stack([me, new_here])[None, :, None, None]
    share = jnp.sum(jnp.where(rou == target, gat, 0.0), axis=-1).reshape(ep * 2 * rows, 1)

    joined = jnp.dot(act, w_in, preferred_element_type=F32)
    hidden = (jax.nn.silu(joined[:, :inner]) * joined[:, inner:]).astype(BF)
    out = jnp.dot(hidden, w_out, preferred_element_type=F32)
    partial = (out * share).astype(BF)
    mix = lax.psum_scatter(partial, "ep", scatter_dimension=0, tiled=True)

    part_rows = feat // grp
    cut = part_rows // ep
    if cut % 32 == 0 and inner % (cut // 2) == 0 and part_rows % LANES == 0 == inner % 64:
        packed = a2a(pack(w_in, w_out, gi, part_rows, ep))
        gate_up_new, down_proj_new = unpack(a2a(packed[sources_new]), part_rows, inner)
    else:
        half_in = lax.dynamic_slice_in_dim(w_in, gi * part_rows, part_rows, 0)
        half_out = lax.dynamic_slice_in_dim(w_out, gi * part_rows, part_rows, 1)
        spread_in = a2a(half_in.reshape(ep, cut, 2 * inner))
        spread_out = a2a(half_out.reshape(ep, inner // ep, part_rows))
        gate_up_new = a2a(spread_in[sources_new]).reshape(part_rows, 2 * inner)
        down_proj_new = a2a(spread_out[sources_new]).reshape(inner, part_rows)

    own = jnp.concatenate([tokens_one, tokens_two], axis=0)
    hidden_all = (own.astype(F32) + mix.astype(F32)).astype(BF)
    normed = rms_norm(hidden_all, norm_gain)
    blocks = [jnp.dot(normed, w, preferred_element_type=F32).astype(BF) for w in kv_blocks]
    kv = jnp.take(jnp.stack(blocks), gi ^ jnp.arange(grp), axis=0)
    kv = kv.transpose(1, 0, 2).reshape(2 * rows, -1)
    return (
        hidden_all[:rows],
        kv[:rows],
        hidden_all[rows:],
        kv[rows:],
        gate_up_new[None],
        down_proj_new[None],
    )


def solution(mesh):
    tok = P(("grp", "ep"), None)
    return jax.shard_map(
        local,
        mesh=mesh,
        in_specs=(
            tok,
            tok,
            tok,
            tok,
            tok,
            tok,
            P(),
            P(),
            P("ep", None, None),
            P("ep", None, None),
            P(),
            P(None, "grp"),
        ),
        out_specs=(tok, tok, tok, tok, P("ep", "grp", None), P("ep", None, "grp")),
        check_vma=False,
    )
```

```python
import jax
import jax.numpy as jnp
from jax import lax
from jax.experimental import pallas as pl
from jax.experimental.pallas import tpu as pltpu
from jax.sharding import PartitionSpec as P

TOP = 6
LANES = 128
BF = jnp.bfloat16
F32 = jnp.float32


def rms_norm(hidden, norm_gain):
    values = hidden.astype(F32)
    inverse_rms = lax.rsqrt(jnp.mean(values * values, axis=-1, keepdims=True) + 1e-06)
    return (values * inverse_rms * norm_gain.astype(F32)).astype(BF)


def swap(x, axis, distance):
    size = lax.axis_size(axis)
    return lax.ppermute(x, axis, [(i, i ^ distance) for i in range(size)])


def join(parts):
    rows, feat = parts[0][0].shape

    def body(*refs):
        out = refs[-1]
        for i in range(len(parts)):
            tok, gat, rou = refs[3 * i : 3 * i + 3]
            out[i * rows : (i + 1) * rows, :feat] = tok[...]
            pad = jnp.zeros((rows, LANES - 2 * TOP), F32)
            more = jnp.concatenate([gat[...].astype(F32), rou[...].astype(F32), pad], axis=1)
            out[i * rows : (i + 1) * rows, feat:] = more.astype(BF)

    shape = (len(parts) * rows, feat + LANES)
    vmem = pl.BlockSpec(memory_space=pltpu.VMEM)
    return pl.pallas_call(
        body,
        name="join",
        out_shape=jax.ShapeDtypeStruct(shape, BF),
        in_specs=[vmem] * (3 * len(parts)),
        out_specs=vmem,
        cost_estimate=pl.CostEstimate(
            flops=0, bytes_accessed=4 * shape[0] * shape[1], transcendentals=0
        ),
    )(*[x for part in parts for x in part])


def experts(rows, target, w_in, w_out, feat):
    inner = w_out.shape[0]
    act = rows[:, :feat]
    gat = rows[:, feat : feat + TOP].astype(F32)
    rou = rows[:, feat + TOP : feat + 2 * TOP].astype(jnp.int32)
    share = jnp.sum(jnp.where(rou == target, gat, 0.0), axis=-1, keepdims=True)
    joined = jnp.dot(act, w_in, preferred_element_type=F32)
    hidden = (jax.nn.silu(joined[:, :inner]) * joined[:, inner:]).astype(BF)
    return jnp.dot(hidden, w_out, preferred_element_type=F32) * share


def a2a(x):
    return lax.all_to_all(x, "ep", split_axis=0, concat_axis=0, tiled=True)


def tiles(piece, pieces, unit, inner, columns):
    per_column = inner // unit
    for j in range(2 * inner // LANES):
        u = j * pieces + piece
        row = pl.multiple_of((u % per_column) * unit, unit)
        column = pl.multiple_of((u // per_column) * LANES, LANES)
        yield row, column, j * LANES


def pack(w_in, w_out, gi, part_rows, pieces):
    inner = w_out.shape[0]
    cut = part_rows // pieces
    unit = cut // 2
    step = 4

    def body(_, gate_ref, down_ref, out_ref):
        at = pl.program_id(0) * step
        for i in range(step):
            out_ref[i, :cut, :] = gate_ref[i * cut : (i + 1) * cut, :]
            for row, column, to in tiles(at + i, pieces, unit, inner, part_rows):
                out_ref[i, cut:, to : to + LANES] = down_ref[pl.ds(row, unit), pl.ds(column, LANES)]

    return pl.pallas_call(
        body,
        name="pack",
        out_shape=jax.ShapeDtypeStruct((pieces, cut + unit, 2 * inner), BF),
        grid_spec=pltpu.PrefetchScalarGridSpec(
            num_scalar_prefetch=1,
            grid=(pieces // step,),
            in_specs=[
                pl.BlockSpec((step * cut, 2 * inner), lambda p, g: (g[0] * (pieces // step) + p, 0)),
                pl.BlockSpec((inner, part_rows), lambda p, g: (0, g[0])),
            ],
            out_specs=pl.BlockSpec((step, cut + unit, 2 * inner), lambda p, g: (p, 0, 0)),
        ),
        compiler_params=pltpu.CompilerParams(vmem_limit_bytes=32 * 1024 * 1024),
        cost_estimate=pl.CostEstimate(
            flops=0, bytes_accessed=12 * part_rows * inner, transcendentals=0
        ),
    )(gi.reshape(1), w_in, w_out)


def unpack(packed, part_rows, inner):
    pieces = packed.shape[0]
    cut = part_rows // pieces
    unit = cut // 2
    step = 4

    def body(in_ref, gate_ref, down_ref):
        at = pl.program_id(0) * step
        for i in range(step):
            gate_ref[i * cut : (i + 1) * cut, :] = in_ref[i, :cut, :]
            for row, column, to in tiles(at + i, pieces, unit, inner, part_rows):
                down_ref[pl.ds(row, unit), pl.ds(column, LANES)] = in_ref[i, cut:, to : to + LANES]

    return pl.pallas_call(
        body,
        name="unpack",
        out_shape=[
            jax.ShapeDtypeStruct((part_rows, 2 * inner), BF),
            jax.ShapeDtypeStruct((inner, part_rows), BF),
        ],
        grid=(pieces // step,),
        in_specs=[pl.BlockSpec((step, cut + unit, 2 * inner), lambda p: (p, 0, 0))],
        out_specs=[
            pl.BlockSpec((step * cut, 2 * inner), lambda p: (p, 0)),
            pl.BlockSpec((inner, part_rows), lambda p: (0, 0)),
        ],
        compiler_params=pltpu.CompilerParams(vmem_limit_bytes=32 * 1024 * 1024),
        cost_estimate=pl.CostEstimate(
            flops=0, bytes_accessed=12 * part_rows * inner, transcendentals=0
        ),
    )(packed)


def local(
    tokens_one,
    routes_one,
    gates_one,
    tokens_two,
    routes_two,
    gates_two,
    old_table,
    new_table,
    gate_up,
    down_proj,
    norm_gain,
    kv_weight,
):
    w_in = gate_up[0]
    w_out = down_proj[0]
    ep = lax.axis_size("ep")
    grp = lax.axis_size("grp")
    me = lax.axis_index("ep")
    gi = lax.axis_index("grp")
    rows = tokens_one.shape[0]
    feat = w_in.shape[0]
    inner = w_out.shape[0]
    numbers = jnp.arange(ep, dtype=jnp.int32)
    sources_new = jnp.sum(
        (new_table[:, None] == old_table[None, :]).astype(jnp.int32) * numbers[None, :], axis=1
    )
    new_here = jnp.sum((sources_new == me).astype(jnp.int32) * numbers)

    mine = join([(tokens_one, gates_one, routes_one), (tokens_two, gates_two, routes_two)])
    far = [4 * i for i in range(1, ep // 4)]
    line = jnp.concatenate([mine] + [swap(mine, "ep", d) for d in far], axis=0)

    part_rows = feat // grp
    cut = part_rows // ep
    line, gi_late = lax.optimization_barrier((line, gi))
    packing = cut % 32 == 0 and inner % (cut // 2) == 0 and part_rows % LANES == 0 == inner % 64
    if packing:
        pieces = [pack(w_in, w_out, gi_late, part_rows, ep)]
    else:
        half_in = lax.dynamic_slice_in_dim(w_in, gi_late * part_rows, part_rows, 0)
        half_out = lax.dynamic_slice_in_dim(w_out, gi_late * part_rows, part_rows, 1)
        pieces = [half_in.reshape(ep, cut, 2 * inner), half_out.reshape(ep, inner // ep, part_rows)]
    spread = [a2a(x) for x in pieces]

    kv_blocks = [lax.optimization_barrier((kv_weight, line))[0]]
    for bit in range(grp.bit_length() - 1):
        kv_blocks = kv_blocks + [swap(x, "grp", 1 << bit) for x in kv_blocks]

    here = jnp.concatenate([line, swap(line, "ep", 2)], axis=0)
    there = swap(here, "ep", 1)
    target = jnp.concatenate([jnp.full((rows, 1), me), jnp.full((rows, 1), new_here)], axis=0)
    target = jnp.tile(target, (ep // 2, 1))
    target, _ = lax.optimization_barrier((target, pieces))
    kept = experts(here, target, w_in, w_out, feat)
    given = experts(there, target, w_in, w_out, feat).astype(BF)

    kept = kept + swap(given, "ep", 1).astype(F32)
    middle = kept.shape[0] // 2
    kept = kept[:middle] + swap(kept[middle:].astype(BF), "ep", 2).astype(F32)
    block = 2 * rows
    mix = kept[:block]
    for i, d in enumerate(far):
        mix = mix + swap(kept[(i + 1) * block : (i + 2) * block].astype(BF), "ep", d).astype(F32)
    own = jnp.concatenate([tokens_one, tokens_two], axis=0)
    hidden_all = (own.astype(F32) + mix).astype(BF)

    hidden_all, wanted = lax.optimization_barrier((hidden_all, sources_new))
    moved = [a2a(x[wanted]) for x in spread]
    if packing:
        gate_up_new, down_proj_new = unpack(moved[0], part_rows, inner)
    else:
        gate_up_new = moved[0].reshape(part_rows, 2 * inner)
        down_proj_new = moved[1].reshape(inner, part_rows)

    normed = rms_norm(hidden_all, norm_gain)
    blocks = [jnp.dot(normed, w, preferred_element_type=F32).astype(BF) for w in kv_blocks]
    kv = jnp.take(jnp.stack(blocks), gi ^ jnp.arange(grp), axis=0)
    kv = kv.transpose(1, 0, 2).reshape(2 * rows, -1)
    return (
        hidden_all[:rows],
        kv[:rows],
        hidden_all[rows:],
        kv[rows:],
        gate_up_new[None],
        down_proj_new[None],
    )


def solution(mesh):
    tok = P(("grp", "ep"), None)
    return jax.shard_map(
        local,
        mesh=mesh,
        in_specs=(
            tok,
            tok,
            tok,
            tok,
            tok,
            tok,
            P(),
            P(),
            P("ep", None, None),
            P("ep", None, None),
            P(),
            P(None, "grp"),
        ),
        out_specs=(tok, tok, tok, tok, P("ep", "grp", None), P("ep", None, "grp")),
        check_vma=False,
    )
```

```python
import jax
import jax.numpy as jnp
from jax import lax
from jax.experimental import pallas as pl
from jax.experimental.pallas import tpu as pltpu
from jax.sharding import PartitionSpec as P

TOP = 6
LANES = 128
BF = jnp.bfloat16
F32 = jnp.float32


def rms_norm(hidden, norm_gain):
    values = hidden.astype(F32)
    inverse_rms = lax.rsqrt(jnp.mean(values * values, axis=-1, keepdims=True) + 1e-06)
    return (values * inverse_rms * norm_gain.astype(F32)).astype(BF)


def swap(x, axis, distance):
    size = lax.axis_size(axis)
    return lax.ppermute(x, axis, [(i, i ^ distance) for i in range(size)])


def join(parts):
    rows, feat = parts[0][0].shape

    def body(*refs):
        out = refs[-1]
        for i in range(len(parts)):
            tok, gat, rou = refs[3 * i : 3 * i + 3]
            out[i * rows : (i + 1) * rows, :feat] = tok[...]
            lane = lax.broadcasted_iota(jnp.int32, (TOP, LANES), 1)
            line = lax.broadcasted_iota(jnp.int32, (TOP, LANES), 0)
            more = sum(
                lax.dot_general(
                    x[...].astype(F32).astype(BF),
                    (lane == line + first).astype(F32).astype(BF),
                    (((0,), (0,)), ((), ())),
                    preferred_element_type=F32,
                )
                for x, first in ((gat, 0), (rou, TOP))
            )
            out[i * rows : (i + 1) * rows, feat:] = more.astype(BF)

    shape = (len(parts) * rows, feat + LANES)
    vmem = pl.BlockSpec(memory_space=pltpu.VMEM)
    return pl.pallas_call(
        body,
        name="join",
        out_shape=jax.ShapeDtypeStruct(shape, BF),
        in_specs=[vmem] * (3 * len(parts)),
        out_specs=vmem,
        cost_estimate=pl.CostEstimate(
            flops=0, bytes_accessed=4 * shape[0] * shape[1], transcendentals=0
        ),
    )(*[x for part in parts for x in part])


def experts(rows, target, w_in, w_out, feat):
    inner = w_out.shape[0]
    act = rows[:, :feat]
    gat = rows[:, feat : feat + TOP].astype(F32)
    rou = rows[:, feat + TOP : feat + 2 * TOP].astype(jnp.int32)
    share = jnp.sum(jnp.where(rou == target, gat, 0.0), axis=-1, keepdims=True)
    joined = jnp.dot(act, w_in, preferred_element_type=F32)
    hidden = (jax.nn.silu(joined[:, :inner]) * joined[:, inner:]).astype(BF)
    return jnp.dot(hidden, w_out, preferred_element_type=F32) * share


def a2a(x):
    return lax.all_to_all(x, "ep", split_axis=0, concat_axis=0, tiled=True)


def tiles(piece, pieces, unit, inner, columns):
    per_column = inner // unit
    for j in range(2 * inner // LANES):
        u = j * pieces + piece
        row = pl.multiple_of((u % per_column) * unit, unit)
        column = pl.multiple_of((u // per_column) * LANES, LANES)
        yield row, column, j * LANES


def pack(w_in, w_out, gi, part_rows, pieces):
    inner = w_out.shape[0]
    cut = part_rows // pieces
    unit = cut // 2
    step = 4

    def body(_, gate_ref, down_ref, out_ref):
        at = pl.program_id(0) * step
        for i in range(step):
            out_ref[i, :cut, :] = gate_ref[i * cut : (i + 1) * cut, :]
            for row, column, to in tiles(at + i, pieces, unit, inner, part_rows):
                out_ref[i, cut:, to : to + LANES] = down_ref[pl.ds(row, unit), pl.ds(column, LANES)]

    return pl.pallas_call(
        body,
        name="pack",
        out_shape=jax.ShapeDtypeStruct((pieces, cut + unit, 2 * inner), BF),
        grid_spec=pltpu.PrefetchScalarGridSpec(
            num_scalar_prefetch=1,
            grid=(pieces // step,),
            in_specs=[
                pl.BlockSpec((step * cut, 2 * inner), lambda p, g: (g[0] * (pieces // step) + p, 0)),
                pl.BlockSpec((inner, part_rows), lambda p, g: (0, g[0])),
            ],
            out_specs=pl.BlockSpec((step, cut + unit, 2 * inner), lambda p, g: (p, 0, 0)),
        ),
        compiler_params=pltpu.CompilerParams(vmem_limit_bytes=32 * 1024 * 1024),
        cost_estimate=pl.CostEstimate(
            flops=0, bytes_accessed=12 * part_rows * inner, transcendentals=0
        ),
    )(gi.reshape(1), w_in, w_out)


def unpack(packed, part_rows, inner):
    pieces = packed.shape[0]
    cut = part_rows // pieces
    unit = cut // 2
    step = 4

    def body(in_ref, gate_ref, down_ref):
        at = pl.program_id(0) * step
        for i in range(step):
            gate_ref[i * cut : (i + 1) * cut, :] = in_ref[i, :cut, :]
            for row, column, to in tiles(at + i, pieces, unit, inner, part_rows):
                down_ref[pl.ds(row, unit), pl.ds(column, LANES)] = in_ref[i, cut:, to : to + LANES]

    return pl.pallas_call(
        body,
        name="unpack",
        out_shape=[
            jax.ShapeDtypeStruct((part_rows, 2 * inner), BF),
            jax.ShapeDtypeStruct((inner, part_rows), BF),
        ],
        grid=(pieces // step,),
        in_specs=[pl.BlockSpec((step, cut + unit, 2 * inner), lambda p: (p, 0, 0))],
        out_specs=[
            pl.BlockSpec((step * cut, 2 * inner), lambda p: (p, 0)),
            pl.BlockSpec((inner, part_rows), lambda p: (0, 0)),
        ],
        compiler_params=pltpu.CompilerParams(vmem_limit_bytes=32 * 1024 * 1024),
        cost_estimate=pl.CostEstimate(
            flops=0, bytes_accessed=12 * part_rows * inner, transcendentals=0
        ),
    )(packed)


def local(
    tokens_one,
    routes_one,
    gates_one,
    tokens_two,
    routes_two,
    gates_two,
    old_table,
    new_table,
    gate_up,
    down_proj,
    norm_gain,
    kv_weight,
):
    w_in = gate_up[0]
    w_out = down_proj[0]
    ep = lax.axis_size("ep")
    grp = lax.axis_size("grp")
    me = lax.axis_index("ep")
    gi = lax.axis_index("grp")
    rows = tokens_one.shape[0]
    feat = w_in.shape[0]
    inner = w_out.shape[0]
    numbers = jnp.arange(ep, dtype=jnp.int32)
    sources_new = jnp.sum(
        (new_table[:, None] == old_table[None, :]).astype(jnp.int32) * numbers[None, :], axis=1
    )
    new_here = jnp.sum((sources_new == me).astype(jnp.int32) * numbers)

    mine = join(
        [(tokens_one, gates_one.T, routes_one.T), (tokens_two, gates_two.T, routes_two.T)]
    )
    far = [4 * i for i in range(1, ep // 4)]
    blocks = [mine] + [swap(mine, "ep", d) for d in far]

    part_rows = feat // grp
    cut = part_rows // ep
    packing = cut % 32 == 0 and inner % (cut // 2) == 0 and part_rows % LANES == 0 == inner % 64
    if packing:
        pieces = [pack(w_in, w_out, gi, part_rows, ep)]
    else:
        half_in = lax.dynamic_slice_in_dim(w_in, gi * part_rows, part_rows, 0)
        half_out = lax.dynamic_slice_in_dim(w_out, gi * part_rows, part_rows, 1)
        pieces = [half_in.reshape(ep, cut, 2 * inner), half_out.reshape(ep, inner // ep, part_rows)]
    near, pieces = lax.optimization_barrier((blocks[1], pieces))
    spread = [a2a(x) for x in pieces]
    line = jnp.concatenate([mine, near] + blocks[2:], axis=0)

    kv_blocks = [lax.optimization_barrier((kv_weight, line))[0]]
    for bit in range(grp.bit_length() - 1):
        kv_blocks = kv_blocks + [swap(x, "grp", 1 << bit) for x in kv_blocks]

    here = jnp.concatenate([line, swap(line, "ep", 2)], axis=0)
    there = swap(here, "ep", 1)
    target = jnp.concatenate([jnp.full((rows, 1), me), jnp.full((rows, 1), new_here)], axis=0)
    target = jnp.tile(target, (ep // 2, 1))
    kept = experts(here, target, w_in, w_out, feat)
    given = experts(there, target, w_in, w_out, feat).astype(BF)

    kept = kept + swap(given, "ep", 1).astype(F32)
    kept, wanted = lax.optimization_barrier((kept, sources_new))
    middle = kept.shape[0] // 2
    kept = kept[:middle] + swap(kept[middle:].astype(BF), "ep", 2).astype(F32)
    block = 2 * rows
    mix = kept[:block]
    for i, d in enumerate(far):
        mix = mix + swap(kept[(i + 1) * block : (i + 2) * block].astype(BF), "ep", d).astype(F32)
    own = jnp.concatenate([tokens_one, tokens_two], axis=0)
    hidden_all = (own.astype(F32) + mix).astype(BF)

    moved = [a2a(x[wanted]) for x in spread]
    if packing:
        gate_up_new, down_proj_new = unpack(moved[0], part_rows, inner)
    else:
        gate_up_new = moved[0].reshape(part_rows, 2 * inner)
        down_proj_new = moved[1].reshape(inner, part_rows)

    normed = rms_norm(hidden_all, norm_gain)
    blocks = [jnp.dot(normed, w, preferred_element_type=F32).astype(BF) for w in kv_blocks]
    kv = jnp.take(jnp.stack(blocks), gi ^ jnp.arange(grp), axis=0)
    kv = kv.transpose(1, 0, 2).reshape(2 * rows, -1)
    return (
        hidden_all[:rows],
        kv[:rows],
        hidden_all[rows:],
        kv[rows:],
        gate_up_new[None],
        down_proj_new[None],
    )


def solution(mesh):
    tok = P(("grp", "ep"), None)
    return jax.shard_map(
        local,
        mesh=mesh,
        in_specs=(
            tok,
            tok,
            tok,
            tok,
            tok,
            tok,
            P(),
            P(),
            P("ep", None, None),
            P("ep", None, None),
            P(),
            P(None, "grp"),
        ),
        out_specs=(tok, tok, tok, tok, P("ep", "grp", None), P("ep", None, "grp")),
        check_vma=False,
    )
```

```python
import jax
import jax.numpy as jnp
from jax import lax
from jax.experimental import pallas as pl
from jax.experimental.pallas import tpu as pltpu
from jax.sharding import PartitionSpec as P

TOP = 6
LANES = 128
BF = jnp.bfloat16
F32 = jnp.float32


def rms_norm(hidden, norm_gain):
    values = hidden.astype(F32)
    inverse_rms = lax.rsqrt(jnp.mean(values * values, axis=-1, keepdims=True) + 1e-06)
    return (values * inverse_rms * norm_gain.astype(F32)).astype(BF)


def swap(x, axis, distance):
    size = lax.axis_size(axis)
    return lax.ppermute(x, axis, [(i, i ^ distance) for i in range(size)])


def join(parts):
    rows, feat = parts[0][0].shape

    def body(*refs):
        out = refs[-1]
        for i in range(len(parts)):
            tok, gat, rou = refs[3 * i : 3 * i + 3]
            out[i * rows : (i + 1) * rows, :feat] = tok[...]
            lane = lax.broadcasted_iota(jnp.int32, (TOP, LANES), 1)
            line = lax.broadcasted_iota(jnp.int32, (TOP, LANES), 0)
            more = sum(
                lax.dot_general(
                    x[...].astype(F32).astype(BF),
                    (lane == line + first).astype(F32).astype(BF),
                    (((0,), (0,)), ((), ())),
                    preferred_element_type=F32,
                )
                for x, first in ((gat, 0), (rou, TOP))
            )
            out[i * rows : (i + 1) * rows, feat:] = more.astype(BF)

    shape = (len(parts) * rows, feat + LANES)
    vmem = pl.BlockSpec(memory_space=pltpu.VMEM)
    return pl.pallas_call(
        body,
        name="join",
        out_shape=jax.ShapeDtypeStruct(shape, BF),
        in_specs=[vmem] * (3 * len(parts)),
        out_specs=vmem,
        cost_estimate=pl.CostEstimate(
            flops=0, bytes_accessed=4 * shape[0] * shape[1], transcendentals=0
        ),
    )(*[x for part in parts for x in part])


def experts(rows, target, w_in, w_out, feat):
    inner = w_out.shape[0]
    act = rows[:, :feat]
    gat = rows[:, feat : feat + TOP].astype(F32)
    rou = rows[:, feat + TOP : feat + 2 * TOP].astype(jnp.int32)
    share = jnp.sum(jnp.where(rou == target, gat, 0.0), axis=-1, keepdims=True)
    joined = jnp.dot(act, w_in, preferred_element_type=F32)
    hidden = (jax.nn.silu(joined[:, :inner]) * joined[:, inner:]).astype(BF)
    return jnp.dot(hidden, w_out, preferred_element_type=F32) * share


def a2a(x):
    return lax.all_to_all(x, "ep", split_axis=0, concat_axis=0, tiled=True)


def tiles(piece, pieces, unit, inner, columns):
    per_column = inner // unit
    for j in range(2 * inner // LANES):
        u = j * pieces + piece
        row = pl.multiple_of((u % per_column) * unit, unit)
        column = pl.multiple_of((u // per_column) * LANES, LANES)
        yield row, column, j * LANES


def pack(w_in, w_out, gi, part_rows, pieces):
    inner = w_out.shape[0]
    cut = part_rows // pieces
    unit = cut // 2
    step = 4

    def body(_, gate_ref, down_ref, out_ref):
        at = pl.program_id(0) * step
        for i in range(step):
            out_ref[i, :cut, :] = gate_ref[i * cut : (i + 1) * cut, :]
            for row, column, to in tiles(at + i, pieces, unit, inner, part_rows):
                out_ref[i, cut:, to : to + LANES] = down_ref[pl.ds(row, unit), pl.ds(column, LANES)]

    return pl.pallas_call(
        body,
        name="pack",
        out_shape=jax.ShapeDtypeStruct((pieces, cut + unit, 2 * inner), BF),
        grid_spec=pltpu.PrefetchScalarGridSpec(
            num_scalar_prefetch=1,
            grid=(pieces // step,),
            in_specs=[
                pl.BlockSpec((step * cut, 2 * inner), lambda p, g: (g[0] * (pieces // step) + p, 0)),
                pl.BlockSpec((inner, part_rows), lambda p, g: (0, g[0])),
            ],
            out_specs=pl.BlockSpec((step, cut + unit, 2 * inner), lambda p, g: (p, 0, 0)),
        ),
        compiler_params=pltpu.CompilerParams(vmem_limit_bytes=32 * 1024 * 1024),
        cost_estimate=pl.CostEstimate(
            flops=0, bytes_accessed=12 * part_rows * inner, transcendentals=0
        ),
    )(gi.reshape(1), w_in, w_out)


def unpack(packed, part_rows, inner):
    pieces = packed.shape[0]
    cut = part_rows // pieces
    unit = cut // 2
    step = 4

    def body(in_ref, gate_ref, down_ref):
        at = pl.program_id(0) * step
        for i in range(step):
            gate_ref[i * cut : (i + 1) * cut, :] = in_ref[i, :cut, :]
            for row, column, to in tiles(at + i, pieces, unit, inner, part_rows):
                down_ref[pl.ds(row, unit), pl.ds(column, LANES)] = in_ref[i, cut:, to : to + LANES]

    return pl.pallas_call(
        body,
        name="unpack",
        out_shape=[
            jax.ShapeDtypeStruct((part_rows, 2 * inner), BF),
            jax.ShapeDtypeStruct((inner, part_rows), BF),
        ],
        grid=(pieces // step,),
        in_specs=[pl.BlockSpec((step, cut + unit, 2 * inner), lambda p: (p, 0, 0))],
        out_specs=[
            pl.BlockSpec((step * cut, 2 * inner), lambda p: (p, 0)),
            pl.BlockSpec((inner, part_rows), lambda p: (0, 0)),
        ],
        compiler_params=pltpu.CompilerParams(vmem_limit_bytes=32 * 1024 * 1024),
        cost_estimate=pl.CostEstimate(
            flops=0, bytes_accessed=12 * part_rows * inner, transcendentals=0
        ),
    )(packed)


def local(
    tokens_one,
    routes_one,
    gates_one,
    tokens_two,
    routes_two,
    gates_two,
    old_table,
    new_table,
    gate_up,
    down_proj,
    norm_gain,
    kv_weight,
):
    w_in = gate_up[0]
    w_out = down_proj[0]
    ep = lax.axis_size("ep")
    grp = lax.axis_size("grp")
    me = lax.axis_index("ep")
    gi = lax.axis_index("grp")
    rows = tokens_one.shape[0]
    feat = w_in.shape[0]
    inner = w_out.shape[0]
    numbers = jnp.arange(ep, dtype=jnp.int32)
    sources_new = jnp.sum(
        (new_table[:, None] == old_table[None, :]).astype(jnp.int32) * numbers[None, :], axis=1
    )
    new_here = jnp.sum((sources_new == me).astype(jnp.int32) * numbers)

    mine = join(
        [(tokens_one, gates_one.T, routes_one.T), (tokens_two, gates_two.T, routes_two.T)]
    )
    far = [4 * i for i in range(1, ep // 4)]
    blocks = [mine] + [swap(mine, "ep", d) for d in far]

    part_rows = feat // grp
    cut = part_rows // ep
    packing = cut % 32 == 0 and inner % (cut // 2) == 0 and part_rows % LANES == 0 == inner % 64
    if packing:
        pieces = [pack(w_in, w_out, gi, part_rows, ep)]
    else:
        half_in = lax.dynamic_slice_in_dim(w_in, gi * part_rows, part_rows, 0)
        half_out = lax.dynamic_slice_in_dim(w_out, gi * part_rows, part_rows, 1)
        pieces = [half_in.reshape(ep, cut, 2 * inner), half_out.reshape(ep, inner // ep, part_rows)]
    near, pieces = lax.optimization_barrier((blocks[1], pieces))
    spread = [a2a(x) for x in pieces]
    line = jnp.concatenate([mine, near] + blocks[2:], axis=0)

    kv_blocks = [lax.optimization_barrier((kv_weight, line))[0]]
    for bit in range(grp.bit_length() - 1):
        kv_blocks = kv_blocks + [swap(x, "grp", 1 << bit) for x in kv_blocks]

    here = jnp.concatenate([line, swap(line, "ep", 2)], axis=0)
    there = swap(here, "ep", 1)
    target = jnp.concatenate([jnp.full((rows, 1), me), jnp.full((rows, 1), new_here)], axis=0)
    target = jnp.tile(target, (ep // 2, 1))
    kept = experts(here, target, w_in, w_out, feat)
    given = experts(there, target, w_in, w_out, feat).astype(BF)

    kept = kept + swap(given, "ep", 1).astype(F32)
    middle = kept.shape[0] // 2
    kept = kept[:middle] + swap(kept[middle:].astype(BF), "ep", 2).astype(F32)
    kept, wanted = lax.optimization_barrier((kept, sources_new))
    block = 2 * rows
    mix = kept[:block]
    for i, d in enumerate(far):
        mix = mix + swap(kept[(i + 1) * block : (i + 2) * block].astype(BF), "ep", d).astype(F32)
    own = jnp.concatenate([tokens_one, tokens_two], axis=0)
    hidden_all = (own.astype(F32) + mix).astype(BF)

    moved = [a2a(x[wanted]) for x in spread]
    if packing:
        gate_up_new, down_proj_new = unpack(moved[0], part_rows, inner)
    else:
        gate_up_new = moved[0].reshape(part_rows, 2 * inner)
        down_proj_new = moved[1].reshape(inner, part_rows)

    normed = rms_norm(hidden_all, norm_gain)
    blocks = [jnp.dot(normed, w, preferred_element_type=F32).astype(BF) for w in kv_blocks]
    kv = jnp.take(jnp.stack(blocks), gi ^ jnp.arange(grp), axis=0)
    kv = kv.transpose(1, 0, 2).reshape(2 * rows, -1)
    return (
        hidden_all[:rows],
        kv[:rows],
        hidden_all[rows:],
        kv[rows:],
        gate_up_new[None],
        down_proj_new[None],
    )


def solution(mesh):
    tok = P(("grp", "ep"), None)
    return jax.shard_map(
        local,
        mesh=mesh,
        in_specs=(
            tok,
            tok,
            tok,
            tok,
            tok,
            tok,
            P(),
            P(),
            P("ep", None, None),
            P("ep", None, None),
            P(),
            P(None, "grp"),
        ),
        out_specs=(tok, tok, tok, tok, P("ep", "grp", None), P("ep", None, "grp")),
        check_vma=False,
    )
```

```python
import jax
import jax.numpy as jnp
from jax import lax
from jax.experimental import pallas as pl
from jax.experimental.pallas import tpu as pltpu
from jax.sharding import PartitionSpec as P

TOP = 6
LANES = 128
BF = jnp.bfloat16
F32 = jnp.float32


def rms_norm(hidden, norm_gain):
    values = hidden.astype(F32)
    inverse_rms = lax.rsqrt(jnp.mean(values * values, axis=-1, keepdims=True) + 1e-06)
    return (values * inverse_rms * norm_gain.astype(F32)).astype(BF)


def swap(x, axis, distance):
    size = lax.axis_size(axis)
    return lax.ppermute(x, axis, [(i, i ^ distance) for i in range(size)])


def join(parts):
    rows, feat = parts[0][0].shape

    def body(*refs):
        out = refs[-1]
        for i in range(len(parts)):
            tok, gat, rou = refs[3 * i : 3 * i + 3]
            out[i * rows : (i + 1) * rows, :feat] = tok[...]
            lane = lax.broadcasted_iota(jnp.int32, (TOP, LANES), 1)
            line = lax.broadcasted_iota(jnp.int32, (TOP, LANES), 0)
            more = sum(
                lax.dot_general(
                    x[...].astype(F32).astype(BF),
                    (lane == line + first).astype(F32).astype(BF),
                    (((0,), (0,)), ((), ())),
                    preferred_element_type=F32,
                )
                for x, first in ((gat, 0), (rou, TOP))
            )
            out[i * rows : (i + 1) * rows, feat:] = more.astype(BF)

    shape = (len(parts) * rows, feat + LANES)
    vmem = pl.BlockSpec(memory_space=pltpu.VMEM)
    return pl.pallas_call(
        body,
        name="join",
        out_shape=jax.ShapeDtypeStruct(shape, BF),
        in_specs=[vmem] * (3 * len(parts)),
        out_specs=vmem,
        cost_estimate=pl.CostEstimate(
            flops=0, bytes_accessed=4 * shape[0] * shape[1], transcendentals=0
        ),
    )(*[x for part in parts for x in part])


def experts(rows, target, w_in, w_out, feat):
    inner = w_out.shape[0]
    act = rows[:, :feat]
    gat = rows[:, feat : feat + TOP].astype(F32)
    rou = rows[:, feat + TOP : feat + 2 * TOP].astype(jnp.int32)
    share = jnp.sum(jnp.where(rou == target, gat, 0.0), axis=-1, keepdims=True)
    joined = jnp.dot(act, w_in, preferred_element_type=F32)
    hidden = (jax.nn.silu(joined[:, :inner]) * joined[:, inner:]).astype(BF)
    return jnp.dot(hidden, w_out, preferred_element_type=F32) * share


def a2a(x):
    return lax.all_to_all(x, "ep", split_axis=0, concat_axis=0, tiled=True)


def tiles(piece, pieces, unit, inner, columns):
    per_column = inner // unit
    for j in range(2 * inner // LANES):
        u = j * pieces + piece
        row = pl.multiple_of((u % per_column) * unit, unit)
        column = pl.multiple_of((u // per_column) * LANES, LANES)
        yield row, column, j * LANES


def pack(w_in, w_out, gi, part_rows, pieces):
    inner = w_out.shape[0]
    cut = part_rows // pieces
    unit = cut // 2
    step = 4

    def body(_, gate_ref, down_ref, out_ref):
        at = pl.program_id(0) * step
        for i in range(step):
            out_ref[i, :cut, :] = gate_ref[i * cut : (i + 1) * cut, :]
            for row, column, to in tiles(at + i, pieces, unit, inner, part_rows):
                out_ref[i, cut:, to : to + LANES] = down_ref[pl.ds(row, unit), pl.ds(column, LANES)]

    return pl.pallas_call(
        body,
        name="pack",
        out_shape=jax.ShapeDtypeStruct((pieces, cut + unit, 2 * inner), BF),
        grid_spec=pltpu.PrefetchScalarGridSpec(
            num_scalar_prefetch=1,
            grid=(pieces // step,),
            in_specs=[
                pl.BlockSpec((step * cut, 2 * inner), lambda p, g: (g[0] * (pieces // step) + p, 0)),
                pl.BlockSpec((inner, part_rows), lambda p, g: (0, g[0])),
            ],
            out_specs=pl.BlockSpec((step, cut + unit, 2 * inner), lambda p, g: (p, 0, 0)),
        ),
        compiler_params=pltpu.CompilerParams(vmem_limit_bytes=32 * 1024 * 1024),
        cost_estimate=pl.CostEstimate(
            flops=0, bytes_accessed=12 * part_rows * inner, transcendentals=0
        ),
    )(gi.reshape(1), w_in, w_out)


def unpack(packed, part_rows, inner):
    pieces = packed.shape[0]
    cut = part_rows // pieces
    unit = cut // 2
    step = 4

    def body(in_ref, gate_ref, down_ref):
        at = pl.program_id(0) * step
        for i in range(step):
            gate_ref[i * cut : (i + 1) * cut, :] = in_ref[i, :cut, :]
            for row, column, to in tiles(at + i, pieces, unit, inner, part_rows):
                down_ref[pl.ds(row, unit), pl.ds(column, LANES)] = in_ref[i, cut:, to : to + LANES]

    return pl.pallas_call(
        body,
        name="unpack",
        out_shape=[
            jax.ShapeDtypeStruct((part_rows, 2 * inner), BF),
            jax.ShapeDtypeStruct((inner, part_rows), BF),
        ],
        grid=(pieces // step,),
        in_specs=[pl.BlockSpec((step, cut + unit, 2 * inner), lambda p: (p, 0, 0))],
        out_specs=[
            pl.BlockSpec((step * cut, 2 * inner), lambda p: (p, 0)),
            pl.BlockSpec((inner, part_rows), lambda p: (0, 0)),
        ],
        compiler_params=pltpu.CompilerParams(vmem_limit_bytes=32 * 1024 * 1024),
        cost_estimate=pl.CostEstimate(
            flops=0, bytes_accessed=12 * part_rows * inner, transcendentals=0
        ),
    )(packed)


def local(
    tokens_one,
    routes_one,
    gates_one,
    tokens_two,
    routes_two,
    gates_two,
    old_table,
    new_table,
    gate_up,
    down_proj,
    norm_gain,
    kv_weight,
):
    w_in = gate_up[0]
    w_out = down_proj[0]
    ep = lax.axis_size("ep")
    grp = lax.axis_size("grp")
    me = lax.axis_index("ep")
    gi = lax.axis_index("grp")
    rows = tokens_one.shape[0]
    feat = w_in.shape[0]
    inner = w_out.shape[0]
    numbers = jnp.arange(ep, dtype=jnp.int32)
    sources_new = jnp.sum(
        (new_table[:, None] == old_table[None, :]).astype(jnp.int32) * numbers[None, :], axis=1
    )
    new_here = jnp.sum((sources_new == me).astype(jnp.int32) * numbers)

    mine = join(
        [(tokens_one, gates_one.T, routes_one.T), (tokens_two, gates_two.T, routes_two.T)]
    )
    across = [[r + 4 * i for i in range(ep // 4)] for r in range(4)]
    inside = [[4 * i + r for r in range(4)] for i in range(ep // 4)]
    everyone = lax.all_gather(mine, "ep", axis_index_groups=across, axis=0, tiled=True)
    everyone = lax.all_gather(everyone, "ep", axis_index_groups=inside, axis=0, tiled=True)

    part_rows = feat // grp
    cut = part_rows // ep
    packing = cut % 32 == 0 and inner % (cut // 2) == 0 and part_rows % LANES == 0 == inner % 64
    if packing:
        pieces = [pack(w_in, w_out, gi, part_rows, ep)]
    else:
        half_in = lax.dynamic_slice_in_dim(w_in, gi * part_rows, part_rows, 0)
        half_out = lax.dynamic_slice_in_dim(w_out, gi * part_rows, part_rows, 1)
        pieces = [half_in.reshape(ep, cut, 2 * inner), half_out.reshape(ep, inner // ep, part_rows)]
    spread = [a2a(x) for x in pieces]

    kv_blocks = [kv_weight]
    for bit in range(grp.bit_length() - 1):
        kv_blocks = kv_blocks + [swap(x, "grp", 1 << bit) for x in kv_blocks]

    target = jnp.concatenate([jnp.full((rows, 1), me), jnp.full((rows, 1), new_here)], axis=0)
    target = jnp.tile(target, (ep, 1))
    mix = experts(everyone, target, w_in, w_out, feat).astype(BF)
    for groups in (inside, across):
        mix = lax.psum_scatter(
            mix, "ep", scatter_dimension=0, axis_index_groups=groups, tiled=True
        )
    own = jnp.concatenate([tokens_one, tokens_two], axis=0)
    hidden_all = (own.astype(F32) + mix.astype(F32)).astype(BF)

    moved = [a2a(x[sources_new]) for x in spread]
    if packing:
        gate_up_new, down_proj_new = unpack(moved[0], part_rows, inner)
    else:
        gate_up_new = moved[0].reshape(part_rows, 2 * inner)
        down_proj_new = moved[1].reshape(inner, part_rows)

    normed = rms_norm(hidden_all, norm_gain)
    blocks = [jnp.dot(normed, w, preferred_element_type=F32).astype(BF) for w in kv_blocks]
    kv = jnp.take(jnp.stack(blocks), gi ^ jnp.arange(grp), axis=0)
    kv = kv.transpose(1, 0, 2).reshape(2 * rows, -1)
    return (
        hidden_all[:rows],
        kv[:rows],
        hidden_all[rows:],
        kv[rows:],
        gate_up_new[None],
        down_proj_new[None],
    )


def solution(mesh):
    tok = P(("grp", "ep"), None)
    return jax.shard_map(
        local,
        mesh=mesh,
        in_specs=(
            tok,
            tok,
            tok,
            tok,
            tok,
            tok,
            P(),
            P(),
            P("ep", None, None),
            P("ep", None, None),
            P(),
            P(None, "grp"),
        ),
        out_specs=(tok, tok, tok, tok, P("ep", "grp", None), P("ep", None, "grp")),
        check_vma=False,
    )
```

```python
import jax
import jax.numpy as jnp
from jax import lax
from jax.experimental import pallas as pl
from jax.experimental.pallas import tpu as pltpu
from jax.sharding import PartitionSpec as P

TOP = 6
LANES = 128
BF = jnp.bfloat16
F32 = jnp.float32


def rms_norm(hidden, norm_gain):
    values = hidden.astype(F32)
    inverse_rms = lax.rsqrt(jnp.mean(values * values, axis=-1, keepdims=True) + 1e-06)
    return (values * inverse_rms * norm_gain.astype(F32)).astype(BF)


def swap(x, axis, distance):
    size = lax.axis_size(axis)
    return lax.ppermute(x, axis, [(i, i ^ distance) for i in range(size)])


def join(parts):
    rows, feat = parts[0][0].shape

    def body(*refs):
        out = refs[-1]
        for i in range(len(parts)):
            tok, gat, rou = refs[3 * i : 3 * i + 3]
            out[i * rows : (i + 1) * rows, :feat] = tok[...]
            lane = lax.broadcasted_iota(jnp.int32, (TOP, LANES), 1)
            line = lax.broadcasted_iota(jnp.int32, (TOP, LANES), 0)
            more = sum(
                lax.dot_general(
                    x[...].astype(F32).astype(BF),
                    (lane == line + first).astype(F32).astype(BF),
                    (((0,), (0,)), ((), ())),
                    preferred_element_type=F32,
                )
                for x, first in ((gat, 0), (rou, TOP))
            )
            out[i * rows : (i + 1) * rows, feat:] = more.astype(BF)

    shape = (len(parts) * rows, feat + LANES)
    vmem = pl.BlockSpec(memory_space=pltpu.VMEM)
    return pl.pallas_call(
        body,
        name="join",
        out_shape=jax.ShapeDtypeStruct(shape, BF),
        in_specs=[vmem] * (3 * len(parts)),
        out_specs=vmem,
        cost_estimate=pl.CostEstimate(
            flops=0, bytes_accessed=4 * shape[0] * shape[1], transcendentals=0
        ),
    )(*[x for part in parts for x in part])


def experts(rows, target, w_in, w_out, feat):
    inner = w_out.shape[0]
    act = rows[:, :feat]
    gat = rows[:, feat : feat + TOP].astype(F32)
    rou = rows[:, feat + TOP : feat + 2 * TOP].astype(jnp.int32)
    share = jnp.sum(jnp.where(rou == target, gat, 0.0), axis=-1, keepdims=True)
    joined = jnp.dot(act, w_in, preferred_element_type=F32)
    hidden = (jax.nn.silu(joined[:, :inner]) * joined[:, inner:]).astype(BF)
    return jnp.dot(hidden, w_out, preferred_element_type=F32) * share


def a2a(x):
    return lax.all_to_all(x, "ep", split_axis=0, concat_axis=0, tiled=True)


def tiles(piece, pieces, unit, inner, columns):
    per_column = inner // unit
    for j in range(2 * inner // LANES):
        u = j * pieces + piece
        row = pl.multiple_of((u % per_column) * unit, unit)
        column = pl.multiple_of((u // per_column) * LANES, LANES)
        yield row, column, j * LANES


def pack(w_in, w_out, gi, part_rows, pieces):
    inner = w_out.shape[0]
    cut = part_rows // pieces
    unit = cut // 2
    step = 4

    def body(_, gate_ref, down_ref, out_ref):
        at = pl.program_id(0) * step
        for i in range(step):
            out_ref[i, :cut, :] = gate_ref[i * cut : (i + 1) * cut, :]
            for row, column, to in tiles(at + i, pieces, unit, inner, part_rows):
                out_ref[i, cut:, to : to + LANES] = down_ref[pl.ds(row, unit), pl.ds(column, LANES)]

    return pl.pallas_call(
        body,
        name="pack",
        out_shape=jax.ShapeDtypeStruct((pieces, cut + unit, 2 * inner), BF),
        grid_spec=pltpu.PrefetchScalarGridSpec(
            num_scalar_prefetch=1,
            grid=(pieces // step,),
            in_specs=[
                pl.BlockSpec((step * cut, 2 * inner), lambda p, g: (g[0] * (pieces // step) + p, 0)),
                pl.BlockSpec((inner, part_rows), lambda p, g: (0, g[0])),
            ],
            out_specs=pl.BlockSpec((step, cut + unit, 2 * inner), lambda p, g: (p, 0, 0)),
        ),
        compiler_params=pltpu.CompilerParams(vmem_limit_bytes=32 * 1024 * 1024),
        cost_estimate=pl.CostEstimate(
            flops=0, bytes_accessed=12 * part_rows * inner, transcendentals=0
        ),
    )(gi.reshape(1), w_in, w_out)


def regroup(packed, index, first, filled=None):
    pieces = packed.shape[0]
    block = (1,) + packed.shape[1:]
    operands = [index, packed] if filled is None else [index, packed, filled]

    def body(*refs):
        refs[-1][...] = refs[1][...]

    return pl.pallas_call(
        body,
        name="regroup",
        out_shape=jax.ShapeDtypeStruct(packed.shape, BF),
        grid_spec=pltpu.PrefetchScalarGridSpec(
            num_scalar_prefetch=1,
            grid=(pieces // 2,),
            in_specs=[pl.BlockSpec(block, lambda i, s: (s[first + i], 0, 0))]
            + [pl.BlockSpec(memory_space=pl.ANY)] * (len(operands) - 2),
            out_specs=pl.BlockSpec(block, lambda i, s: (first + i, 0, 0)),
        ),
        input_output_aliases={} if filled is None else {2: 0},
        cost_estimate=pl.CostEstimate(flops=0, bytes_accessed=400_000_000, transcendentals=0),
    )(*operands)


def unpack(packed, part_rows, inner):
    pieces = packed.shape[0]
    cut = part_rows // pieces
    unit = cut // 2
    step = 4

    def body(in_ref, gate_ref, down_ref):
        at = pl.program_id(0) * step
        for i in range(step):
            gate_ref[i * cut : (i + 1) * cut, :] = in_ref[i, :cut, :]
            for row, column, to in tiles(at + i, pieces, unit, inner, part_rows):
                down_ref[pl.ds(row, unit), pl.ds(column, LANES)] = in_ref[i, cut:, to : to + LANES]

    return pl.pallas_call(
        body,
        name="unpack",
        out_shape=[
            jax.ShapeDtypeStruct((part_rows, 2 * inner), BF),
            jax.ShapeDtypeStruct((inner, part_rows), BF),
        ],
        grid=(pieces // step,),
        in_specs=[pl.BlockSpec((step, cut + unit, 2 * inner), lambda p: (p, 0, 0))],
        out_specs=[
            pl.BlockSpec((step * cut, 2 * inner), lambda p: (p, 0)),
            pl.BlockSpec((inner, part_rows), lambda p: (0, 0)),
        ],
        compiler_params=pltpu.CompilerParams(vmem_limit_bytes=32 * 1024 * 1024),
        cost_estimate=pl.CostEstimate(
            flops=0, bytes_accessed=12 * part_rows * inner, transcendentals=0
        ),
    )(packed)


def local(
    tokens_one,
    routes_one,
    gates_one,
    tokens_two,
    routes_two,
    gates_two,
    old_table,
    new_table,
    gate_up,
    down_proj,
    norm_gain,
    kv_weight,
):
    w_in = gate_up[0]
    w_out = down_proj[0]
    ep = lax.axis_size("ep")
    grp = lax.axis_size("grp")
    me = lax.axis_index("ep")
    gi = lax.axis_index("grp")
    rows = tokens_one.shape[0]
    feat = w_in.shape[0]
    inner = w_out.shape[0]
    numbers = jnp.arange(ep, dtype=jnp.int32)
    sources_new = jnp.sum(
        (new_table[:, None] == old_table[None, :]).astype(jnp.int32) * numbers[None, :], axis=1
    )
    new_here = jnp.sum((sources_new == me).astype(jnp.int32) * numbers)

    mine = join(
        [(tokens_one, gates_one.T, routes_one.T), (tokens_two, gates_two.T, routes_two.T)]
    )
    far = [4 * i for i in range(1, ep // 4)]
    blocks = [mine] + [swap(mine, "ep", d) for d in far]

    part_rows = feat // grp
    cut = part_rows // ep
    packing = cut % 32 == 0 and inner % (cut // 2) == 0 and part_rows % LANES == 0 == inner % 64
    if packing:
        pieces = [pack(w_in, w_out, gi, part_rows, ep)]
    else:
        half_in = lax.dynamic_slice_in_dim(w_in, gi * part_rows, part_rows, 0)
        half_out = lax.dynamic_slice_in_dim(w_out, gi * part_rows, part_rows, 1)
        pieces = [half_in.reshape(ep, cut, 2 * inner), half_out.reshape(ep, inner // ep, part_rows)]
    near, pieces = lax.optimization_barrier((blocks[1], pieces))
    spread = [a2a(x) for x in pieces]
    line = jnp.concatenate([mine, near] + blocks[2:], axis=0)

    kv_blocks = [lax.optimization_barrier((kv_weight, line))[0]]
    for bit in range(grp.bit_length() - 1):
        kv_blocks = kv_blocks + [swap(x, "grp", 1 << bit) for x in kv_blocks]

    here = jnp.concatenate([line, swap(line, "ep", 2)], axis=0)
    there = swap(here, "ep", 1)
    target = jnp.concatenate([jnp.full((rows, 1), me), jnp.full((rows, 1), new_here)], axis=0)
    target = jnp.tile(target, (ep // 2, 1))
    kept = experts(here, target, w_in, w_out, feat)
    given = experts(there, target, w_in, w_out, feat).astype(BF)

    kept = kept + swap(given, "ep", 1).astype(F32)
    middle = kept.shape[0] // 2
    sent, wanted = lax.optimization_barrier((kept[middle:].astype(BF), sources_new))
    halves = [regroup(x, wanted, 0) for x in spread]
    kept = kept[:middle] + swap(sent, "ep", 2).astype(F32)
    block = 2 * rows
    sent = [kept[(i + 1) * block : (i + 2) * block].astype(BF) for i in range(len(far))]
    sent, wanted = lax.optimization_barrier((sent, wanted))
    came = [swap(x, "ep", d) for x, d in zip(sent, far)]
    grouped = [regroup(x, wanted, ep // 2, y) for x, y in zip(spread, halves)]
    came, grouped = lax.optimization_barrier((came, grouped))
    moved = [a2a(x) for x in grouped]
    mix = kept[:block] + sum(x.astype(F32) for x in came)
    own = jnp.concatenate([tokens_one, tokens_two], axis=0)
    hidden_all = (own.astype(F32) + mix).astype(BF)

    if packing:
        gate_up_new, down_proj_new = unpack(moved[0], part_rows, inner)
    else:
        gate_up_new = moved[0].reshape(part_rows, 2 * inner)
        down_proj_new = moved[1].reshape(inner, part_rows)

    normed = rms_norm(hidden_all, norm_gain)
    blocks = [jnp.dot(normed, w, preferred_element_type=F32).astype(BF) for w in kv_blocks]
    kv = jnp.take(jnp.stack(blocks), gi ^ jnp.arange(grp), axis=0)
    kv = kv.transpose(1, 0, 2).reshape(2 * rows, -1)
    return (
        hidden_all[:rows],
        kv[:rows],
        hidden_all[rows:],
        kv[rows:],
        gate_up_new[None],
        down_proj_new[None],
    )


def solution(mesh):
    tok = P(("grp", "ep"), None)
    return jax.shard_map(
        local,
        mesh=mesh,
        in_specs=(
            tok,
            tok,
            tok,
            tok,
            tok,
            tok,
            P(),
            P(),
            P("ep", None, None),
            P("ep", None, None),
            P(),
            P(None, "grp"),
        ),
        out_specs=(tok, tok, tok, tok, P("ep", "grp", None), P("ep", None, "grp")),
        check_vma=False,
    )
```

```python
import jax
import jax.numpy as jnp
from jax import lax
from jax.experimental import pallas as pl
from jax.experimental.pallas import tpu as pltpu
from jax.sharding import PartitionSpec as P

TOP = 6
LANES = 128
BF = jnp.bfloat16
F32 = jnp.float32


def rms_norm(hidden, norm_gain):
    values = hidden.astype(F32)
    inverse_rms = lax.rsqrt(jnp.mean(values * values, axis=-1, keepdims=True) + 1e-06)
    return (values * inverse_rms * norm_gain.astype(F32)).astype(BF)


def swap(x, axis, distance):
    size = lax.axis_size(axis)
    return lax.ppermute(x, axis, [(i, i ^ distance) for i in range(size)])


def join(parts):
    rows, feat = parts[0][0].shape

    def body(*refs):
        out = refs[-1]
        for i in range(len(parts)):
            tok, gat, rou = refs[3 * i : 3 * i + 3]
            out[i * rows : (i + 1) * rows, :feat] = tok[...]
            lane = lax.broadcasted_iota(jnp.int32, (TOP, LANES), 1)
            line = lax.broadcasted_iota(jnp.int32, (TOP, LANES), 0)
            more = sum(
                lax.dot_general(
                    x[...].astype(F32).astype(BF),
                    (lane == line + first).astype(F32).astype(BF),
                    (((0,), (0,)), ((), ())),
                    preferred_element_type=F32,
                )
                for x, first in ((gat, 0), (rou, TOP))
            )
            out[i * rows : (i + 1) * rows, feat:] = more.astype(BF)

    shape = (len(parts) * rows, feat + LANES)
    vmem = pl.BlockSpec(memory_space=pltpu.VMEM)
    return pl.pallas_call(
        body,
        name="join",
        out_shape=jax.ShapeDtypeStruct(shape, BF),
        in_specs=[vmem] * (3 * len(parts)),
        out_specs=vmem,
        cost_estimate=pl.CostEstimate(
            flops=0, bytes_accessed=4 * shape[0] * shape[1], transcendentals=0
        ),
    )(*[x for part in parts for x in part])


def experts(rows, target, w_in, w_out, feat):
    inner = w_out.shape[0]
    act = rows[:, :feat]
    gat = rows[:, feat : feat + TOP].astype(F32)
    rou = rows[:, feat + TOP : feat + 2 * TOP].astype(jnp.int32)
    share = jnp.sum(jnp.where(rou == target, gat, 0.0), axis=-1, keepdims=True)
    joined = jnp.dot(act, w_in, preferred_element_type=F32)
    hidden = (jax.nn.silu(joined[:, :inner]) * joined[:, inner:]).astype(BF)
    return jnp.dot(hidden, w_out, preferred_element_type=F32) * share


def a2a(x):
    return lax.all_to_all(x, "ep", split_axis=0, concat_axis=0, tiled=True)


def tiles(piece, pieces, unit, inner, columns):
    per_column = inner // unit
    for j in range(2 * inner // LANES):
        u = j * pieces + piece
        row = pl.multiple_of((u % per_column) * unit, unit)
        column = pl.multiple_of((u // per_column) * LANES, LANES)
        yield row, column, j * LANES


def pack(w_in, w_out, gi, part_rows, pieces):
    inner = w_out.shape[0]
    cut = part_rows // pieces
    unit = cut // 2
    step = 4

    def body(_, gate_ref, down_ref, out_ref):
        at = pl.program_id(0) * step
        for i in range(step):
            out_ref[i, :cut, :] = gate_ref[i * cut : (i + 1) * cut, :]
            for row, column, to in tiles(at + i, pieces, unit, inner, part_rows):
                out_ref[i, cut:, to : to + LANES] = down_ref[pl.ds(row, unit), pl.ds(column, LANES)]

    return pl.pallas_call(
        body,
        name="pack",
        out_shape=jax.ShapeDtypeStruct((pieces, cut + unit, 2 * inner), BF),
        grid_spec=pltpu.PrefetchScalarGridSpec(
            num_scalar_prefetch=1,
            grid=(pieces // step,),
            in_specs=[
                pl.BlockSpec((step * cut, 2 * inner), lambda p, g: (g[0] * (pieces // step) + p, 0)),
                pl.BlockSpec((inner, part_rows), lambda p, g: (0, g[0])),
            ],
            out_specs=pl.BlockSpec((step, cut + unit, 2 * inner), lambda p, g: (p, 0, 0)),
        ),
        compiler_params=pltpu.CompilerParams(vmem_limit_bytes=32 * 1024 * 1024),
        cost_estimate=pl.CostEstimate(
            flops=0, bytes_accessed=12 * part_rows * inner, transcendentals=0
        ),
    )(gi.reshape(1), w_in, w_out)


def marker(arrived, index):
    def body(*refs):
        refs[-1][...] = refs[0][...]

    vmem = pl.BlockSpec(memory_space=pltpu.VMEM)
    return pl.pallas_call(
        body,
        name="marker",
        out_shape=jax.ShapeDtypeStruct(index.shape, index.dtype),
        in_specs=[vmem] + [pl.BlockSpec(memory_space=pl.ANY)] * len(arrived),
        out_specs=vmem,
        cost_estimate=pl.CostEstimate(flops=0, bytes_accessed=400_000_000, transcendentals=0),
    )(index, *arrived)


def unpack(packed, part_rows, inner):
    pieces = packed.shape[0]
    cut = part_rows // pieces
    unit = cut // 2
    step = 4

    def body(in_ref, gate_ref, down_ref):
        at = pl.program_id(0) * step
        for i in range(step):
            gate_ref[i * cut : (i + 1) * cut, :] = in_ref[i, :cut, :]
            for row, column, to in tiles(at + i, pieces, unit, inner, part_rows):
                down_ref[pl.ds(row, unit), pl.ds(column, LANES)] = in_ref[i, cut:, to : to + LANES]

    return pl.pallas_call(
        body,
        name="unpack",
        out_shape=[
            jax.ShapeDtypeStruct((part_rows, 2 * inner), BF),
            jax.ShapeDtypeStruct((inner, part_rows), BF),
        ],
        grid=(pieces // step,),
        in_specs=[pl.BlockSpec((step, cut + unit, 2 * inner), lambda p: (p, 0, 0))],
        out_specs=[
            pl.BlockSpec((step * cut, 2 * inner), lambda p: (p, 0)),
            pl.BlockSpec((inner, part_rows), lambda p: (0, 0)),
        ],
        compiler_params=pltpu.CompilerParams(vmem_limit_bytes=32 * 1024 * 1024),
        cost_estimate=pl.CostEstimate(
            flops=0, bytes_accessed=12 * part_rows * inner, transcendentals=0
        ),
    )(packed)


def local(
    tokens_one,
    routes_one,
    gates_one,
    tokens_two,
    routes_two,
    gates_two,
    old_table,
    new_table,
    gate_up,
    down_proj,
    norm_gain,
    kv_weight,
):
    w_in = gate_up[0]
    w_out = down_proj[0]
    ep = lax.axis_size("ep")
    grp = lax.axis_size("grp")
    me = lax.axis_index("ep")
    gi = lax.axis_index("grp")
    rows = tokens_one.shape[0]
    feat = w_in.shape[0]
    inner = w_out.shape[0]
    numbers = jnp.arange(ep, dtype=jnp.int32)
    sources_new = jnp.sum(
        (new_table[:, None] == old_table[None, :]).astype(jnp.int32) * numbers[None, :], axis=1
    )
    new_here = jnp.sum((sources_new == me).astype(jnp.int32) * numbers)

    mine = join(
        [(tokens_one, gates_one.T, routes_one.T), (tokens_two, gates_two.T, routes_two.T)]
    )
    far = [4 * i for i in range(1, ep // 4)]
    blocks = [mine] + [swap(mine, "ep", d) for d in far]

    part_rows = feat // grp
    cut = part_rows // ep
    packing = cut % 32 == 0 and inner % (cut // 2) == 0 and part_rows % LANES == 0 == inner % 64
    if packing:
        pieces = [pack(w_in, w_out, gi, part_rows, ep)]
    else:
        half_in = lax.dynamic_slice_in_dim(w_in, gi * part_rows, part_rows, 0)
        half_out = lax.dynamic_slice_in_dim(w_out, gi * part_rows, part_rows, 1)
        pieces = [half_in.reshape(ep, cut, 2 * inner), half_out.reshape(ep, inner // ep, part_rows)]
    near, pieces = lax.optimization_barrier((blocks[1], pieces))
    spread = [a2a(x) for x in pieces]
    line = jnp.concatenate([mine, near] + blocks[2:], axis=0)

    kv_blocks = [lax.optimization_barrier((kv_weight, line))[0]]
    for bit in range(grp.bit_length() - 1):
        kv_blocks = kv_blocks + [swap(x, "grp", 1 << bit) for x in kv_blocks]

    here = jnp.concatenate([line, swap(line, "ep", 2)], axis=0)
    there = swap(here, "ep", 1)
    target = jnp.concatenate([jnp.full((rows, 1), me), jnp.full((rows, 1), new_here)], axis=0)
    target = jnp.tile(target, (ep // 2, 1))
    kept = experts(here, target, w_in, w_out, feat)
    given = experts(there, target, w_in, w_out, feat).astype(BF)

    kept = kept + swap(given, "ep", 1).astype(F32)
    middle = kept.shape[0] // 2
    sent, wanted = lax.optimization_barrier((kept[middle:].astype(BF), sources_new))
    wanted = marker(spread, wanted)
    kept = kept[:middle] + swap(sent, "ep", 2).astype(F32)
    kept, wanted = lax.optimization_barrier((kept, wanted))
    block = 2 * rows
    sent = [kept[(i + 1) * block : (i + 2) * block].astype(BF) for i in range(len(far))]
    came = [swap(x, "ep", d) for x, d in zip(sent, far)]
    grouped = [x[wanted] for x in spread]
    came, grouped = lax.optimization_barrier((came, grouped))
    moved = [a2a(x) for x in grouped]
    mix = kept[:block] + sum(x.astype(F32) for x in came)
    own = jnp.concatenate([tokens_one, tokens_two], axis=0)
    hidden_all = (own.astype(F32) + mix).astype(BF)

    if packing:
        gate_up_new, down_proj_new = unpack(moved[0], part_rows, inner)
    else:
        gate_up_new = moved[0].reshape(part_rows, 2 * inner)
        down_proj_new = moved[1].reshape(inner, part_rows)

    normed = rms_norm(hidden_all, norm_gain)
    blocks = [jnp.dot(normed, w, preferred_element_type=F32).astype(BF) for w in kv_blocks]
    kv = jnp.take(jnp.stack(blocks), gi ^ jnp.arange(grp), axis=0)
    kv = kv.transpose(1, 0, 2).reshape(2 * rows, -1)
    return (
        hidden_all[:rows],
        kv[:rows],
        hidden_all[rows:],
        kv[rows:],
        gate_up_new[None],
        down_proj_new[None],
    )


def solution(mesh):
    tok = P(("grp", "ep"), None)
    return jax.shard_map(
        local,
        mesh=mesh,
        in_specs=(
            tok,
            tok,
            tok,
            tok,
            tok,
            tok,
            P(),
            P(),
            P("ep", None, None),
            P("ep", None, None),
            P(),
            P(None, "grp"),
        ),
        out_specs=(tok, tok, tok, tok, P("ep", "grp", None), P("ep", None, "grp")),
        check_vma=False,
    )
```

```python
import jax
import jax.numpy as jnp
from jax import lax
from jax.experimental import pallas as pl
from jax.experimental.pallas import tpu as pltpu
from jax.sharding import PartitionSpec as P

TOP = 6
LANES = 128
BF = jnp.bfloat16
F32 = jnp.float32


def rms_norm(hidden, norm_gain):
    values = hidden.astype(F32)
    inverse_rms = lax.rsqrt(jnp.mean(values * values, axis=-1, keepdims=True) + 1e-06)
    return (values * inverse_rms * norm_gain.astype(F32)).astype(BF)


def swap(x, axis, distance):
    size = lax.axis_size(axis)
    return lax.ppermute(x, axis, [(i, i ^ distance) for i in range(size)])


def join(parts):
    rows, feat = parts[0][0].shape

    def body(*refs):
        out = refs[-1]
        for i in range(len(parts)):
            tok, gat, rou = refs[3 * i : 3 * i + 3]
            out[i * rows : (i + 1) * rows, :feat] = tok[...]
            lane = lax.broadcasted_iota(jnp.int32, (TOP, LANES), 1)
            line = lax.broadcasted_iota(jnp.int32, (TOP, LANES), 0)
            more = sum(
                lax.dot_general(
                    x[...].astype(F32).astype(BF),
                    (lane == line + first).astype(F32).astype(BF),
                    (((0,), (0,)), ((), ())),
                    preferred_element_type=F32,
                )
                for x, first in ((gat, 0), (rou, TOP))
            )
            out[i * rows : (i + 1) * rows, feat:] = more.astype(BF)

    shape = (len(parts) * rows, feat + LANES)
    vmem = pl.BlockSpec(memory_space=pltpu.VMEM)
    return pl.pallas_call(
        body,
        name="join",
        out_shape=jax.ShapeDtypeStruct(shape, BF),
        in_specs=[vmem] * (3 * len(parts)),
        out_specs=vmem,
        cost_estimate=pl.CostEstimate(
            flops=0, bytes_accessed=4 * shape[0] * shape[1], transcendentals=0
        ),
    )(*[x for part in parts for x in part])


def experts(rows, each, targets, w_in, w_out, dtype):
    inner, feat = w_out.shape
    count = rows.shape[0]
    width = rows.shape[1]
    step = min(256, count)

    def body(target_ref, row_ref, in_ref, out_w_ref, out_ref):
        joined = jnp.dot(row_ref[:, :feat], in_ref[...], preferred_element_type=F32)
        upward = pltpu.roll(joined, inner, 1)
        hidden = joined / (1.0 + jnp.exp(-joined)) * upward
        hidden = hidden[:, :inner].astype(BF)
        result = jnp.dot(hidden, out_w_ref[...], preferred_element_type=F32)
        more = row_ref[:, feat:].astype(F32)
        routes = pltpu.roll(more, LANES - TOP, 1)
        lane = lax.broadcasted_iota(jnp.int32, more.shape, 1)
        line = lax.broadcasted_iota(jnp.int32, more.shape, 0)
        target = jnp.where(line % (2 * each) < each, target_ref[0], target_ref[1]).astype(F32)
        chosen = (routes == target) & (lane < TOP)
        share = jnp.sum(jnp.where(chosen, more, 0.0), axis=1, keepdims=True)
        out_ref[...] = (result * share).astype(dtype)

    return pl.pallas_call(
        body,
        name="experts",
        out_shape=jax.ShapeDtypeStruct((count, feat), dtype),
        grid=(count // step,),
        in_specs=[
            pl.BlockSpec(memory_space=pltpu.SMEM),
            pl.BlockSpec((step, width), lambda i: (i, 0)),
            pl.BlockSpec(w_in.shape, lambda i: (0, 0)),
            pl.BlockSpec(w_out.shape, lambda i: (0, 0)),
        ],
        out_specs=pl.BlockSpec((step, feat), lambda i: (i, 0)),
        compiler_params=pltpu.CompilerParams(vmem_limit_bytes=48 * 1024 * 1024),
        cost_estimate=pl.CostEstimate(flops=0, bytes_accessed=0, transcendentals=0),
    )(targets, rows, w_in, w_out)


def a2a(x):
    return lax.all_to_all(x, "ep", split_axis=0, concat_axis=0, tiled=True)


def tiles(piece, pieces, unit, inner, columns):
    per_column = inner // unit
    for j in range(2 * inner // LANES):
        u = j * pieces + piece
        row = pl.multiple_of((u % per_column) * unit, unit)
        column = pl.multiple_of((u // per_column) * LANES, LANES)
        yield row, column, j * LANES


def pack(w_in, w_out, gi, part_rows, pieces):
    inner = w_out.shape[0]
    cut = part_rows // pieces
    unit = cut // 2
    step = 4

    def body(_, gate_ref, down_ref, out_ref):
        at = pl.program_id(0) * step
        for i in range(step):
            out_ref[i, :cut, :] = gate_ref[i * cut : (i + 1) * cut, :]
            for row, column, to in tiles(at + i, pieces, unit, inner, part_rows):
                out_ref[i, cut:, to : to + LANES] = down_ref[pl.ds(row, unit), pl.ds(column, LANES)]

    return pl.pallas_call(
        body,
        name="pack",
        out_shape=jax.ShapeDtypeStruct((pieces, cut + unit, 2 * inner), BF),
        grid_spec=pltpu.PrefetchScalarGridSpec(
            num_scalar_prefetch=1,
            grid=(pieces // step,),
            in_specs=[
                pl.BlockSpec((step * cut, 2 * inner), lambda p, g: (g[0] * (pieces // step) + p, 0)),
                pl.BlockSpec((inner, part_rows), lambda p, g: (0, g[0])),
            ],
            out_specs=pl.BlockSpec((step, cut + unit, 2 * inner), lambda p, g: (p, 0, 0)),
        ),
        compiler_params=pltpu.CompilerParams(vmem_limit_bytes=32 * 1024 * 1024),
        cost_estimate=pl.CostEstimate(
            flops=0, bytes_accessed=12 * part_rows * inner, transcendentals=0
        ),
    )(gi.reshape(1), w_in, w_out)


def unpack(packed, part_rows, inner):
    pieces = packed.shape[0]
    cut = part_rows // pieces
    unit = cut // 2
    step = 4

    def body(in_ref, gate_ref, down_ref):
        at = pl.program_id(0) * step
        for i in range(step):
            gate_ref[i * cut : (i + 1) * cut, :] = in_ref[i, :cut, :]
            for row, column, to in tiles(at + i, pieces, unit, inner, part_rows):
                down_ref[pl.ds(row, unit), pl.ds(column, LANES)] = in_ref[i, cut:, to : to + LANES]

    return pl.pallas_call(
        body,
        name="unpack",
        out_shape=[
            jax.ShapeDtypeStruct((part_rows, 2 * inner), BF),
            jax.ShapeDtypeStruct((inner, part_rows), BF),
        ],
        grid=(pieces // step,),
        in_specs=[pl.BlockSpec((step, cut + unit, 2 * inner), lambda p: (p, 0, 0))],
        out_specs=[
            pl.BlockSpec((step * cut, 2 * inner), lambda p: (p, 0)),
            pl.BlockSpec((inner, part_rows), lambda p: (0, 0)),
        ],
        compiler_params=pltpu.CompilerParams(vmem_limit_bytes=32 * 1024 * 1024),
        cost_estimate=pl.CostEstimate(
            flops=0, bytes_accessed=12 * part_rows * inner, transcendentals=0
        ),
    )(packed)


def local(
    tokens_one,
    routes_one,
    gates_one,
    tokens_two,
    routes_two,
    gates_two,
    old_table,
    new_table,
    gate_up,
    down_proj,
    norm_gain,
    kv_weight,
):
    w_in = gate_up[0]
    w_out = down_proj[0]
    ep = lax.axis_size("ep")
    grp = lax.axis_size("grp")
    me = lax.axis_index("ep")
    gi = lax.axis_index("grp")
    rows = tokens_one.shape[0]
    feat = w_in.shape[0]
    inner = w_out.shape[0]
    numbers = jnp.arange(ep, dtype=jnp.int32)
    sources_new = jnp.sum(
        (new_table[:, None] == old_table[None, :]).astype(jnp.int32) * numbers[None, :], axis=1
    )
    new_here = jnp.sum((sources_new == me).astype(jnp.int32) * numbers)

    mine = join(
        [(tokens_one, gates_one.T, routes_one.T), (tokens_two, gates_two.T, routes_two.T)]
    )
    far = [4 * i for i in range(1, ep // 4)]
    blocks = [mine] + [swap(mine, "ep", d) for d in far]

    part_rows = feat // grp
    cut = part_rows // ep
    packing = cut % 32 == 0 and inner % (cut // 2) == 0 and part_rows % LANES == 0 == inner % 64
    if packing:
        pieces = [pack(w_in, w_out, gi, part_rows, ep)]
    else:
        half_in = lax.dynamic_slice_in_dim(w_in, gi * part_rows, part_rows, 0)
        half_out = lax.dynamic_slice_in_dim(w_out, gi * part_rows, part_rows, 1)
        pieces = [half_in.reshape(ep, cut, 2 * inner), half_out.reshape(ep, inner // ep, part_rows)]
    near, pieces = lax.optimization_barrier((blocks[1], pieces))
    spread = [a2a(x) for x in pieces]
    line = jnp.concatenate([mine, near] + blocks[2:], axis=0)

    kv_blocks = [lax.optimization_barrier((kv_weight, line))[0]]
    for bit in range(grp.bit_length() - 1):
        kv_blocks = kv_blocks + [swap(x, "grp", 1 << bit) for x in kv_blocks]

    here = jnp.concatenate([line, swap(line, "ep", 2)], axis=0)
    there = swap(here, "ep", 1)
    targets = jnp.stack([me, new_here])
    kept = experts(here, rows, targets, w_in, w_out, F32)
    given = experts(there, rows, targets, w_in, w_out, BF)

    kept = kept + swap(given, "ep", 1).astype(F32)
    middle = kept.shape[0] // 2
    sent, wanted = lax.optimization_barrier((kept[middle:].astype(BF), sources_new))
    kept = kept[:middle] + swap(sent, "ep", 2).astype(F32)
    kept, wanted = lax.optimization_barrier((kept, wanted))
    block = 2 * rows
    sent = [kept[(i + 1) * block : (i + 2) * block].astype(BF) for i in range(len(far))]
    came = [swap(x, "ep", d) for x, d in zip(sent, far)]
    grouped = [x[wanted] for x in spread]
    came, grouped = lax.optimization_barrier((came, grouped))
    moved = [a2a(x) for x in grouped]
    mix = kept[:block] + sum(x.astype(F32) for x in came)
    own = jnp.concatenate([tokens_one, tokens_two], axis=0)
    hidden_all = (own.astype(F32) + mix).astype(BF)

    if packing:
        gate_up_new, down_proj_new = unpack(moved[0], part_rows, inner)
    else:
        gate_up_new = moved[0].reshape(part_rows, 2 * inner)
        down_proj_new = moved[1].reshape(inner, part_rows)

    normed = rms_norm(hidden_all, norm_gain)
    blocks = [jnp.dot(normed, w, preferred_element_type=F32).astype(BF) for w in kv_blocks]
    kv = jnp.take(jnp.stack(blocks), gi ^ jnp.arange(grp), axis=0)
    kv = kv.transpose(1, 0, 2).reshape(2 * rows, -1)
    return (
        hidden_all[:rows],
        kv[:rows],
        hidden_all[rows:],
        kv[rows:],
        gate_up_new[None],
        down_proj_new[None],
    )


def solution(mesh):
    tok = P(("grp", "ep"), None)
    return jax.shard_map(
        local,
        mesh=mesh,
        in_specs=(
            tok,
            tok,
            tok,
            tok,
            tok,
            tok,
            P(),
            P(),
            P("ep", None, None),
            P("ep", None, None),
            P(),
            P(None, "grp"),
        ),
        out_specs=(tok, tok, tok, tok, P("ep", "grp", None), P("ep", None, "grp")),
        check_vma=False,
    )
```

```python
import jax
import jax.numpy as jnp
from jax import lax
from jax.experimental import pallas as pl
from jax.experimental.pallas import tpu as pltpu
from jax.sharding import PartitionSpec as P

TOP = 6
LANES = 128
BF = jnp.bfloat16
F32 = jnp.float32


def rms_norm(hidden, norm_gain):
    def body(hidden_ref, gain_ref, out_ref):
        values = hidden_ref[...].astype(F32)
        inverse_rms = lax.rsqrt(jnp.mean(values * values, axis=-1, keepdims=True) + 1e-06)
        out_ref[...] = (values * inverse_rms * gain_ref[...].astype(F32)).astype(BF)

    vmem = pl.BlockSpec(memory_space=pltpu.VMEM)
    return pl.pallas_call(
        body,
        name="rms_norm",
        out_shape=jax.ShapeDtypeStruct(hidden.shape, BF),
        in_specs=[vmem, vmem],
        out_specs=vmem,
        cost_estimate=pl.CostEstimate(flops=0, bytes_accessed=18_000_000, transcendentals=0),
    )(hidden, norm_gain.reshape(1, -1))


def swap(x, axis, distance):
    size = lax.axis_size(axis)
    return lax.ppermute(x, axis, [(i, i ^ distance) for i in range(size)])


def join(parts):
    rows, feat = parts[0][0].shape

    def body(*refs):
        out = refs[-1]
        for i in range(len(parts)):
            tok, gat, rou = refs[3 * i : 3 * i + 3]
            out[i * rows : (i + 1) * rows, :feat] = tok[...]
            lane = lax.broadcasted_iota(jnp.int32, (TOP, LANES), 1)
            line = lax.broadcasted_iota(jnp.int32, (TOP, LANES), 0)
            more = sum(
                lax.dot_general(
                    x[...].astype(F32).astype(BF),
                    (lane == line + first).astype(F32).astype(BF),
                    (((0,), (0,)), ((), ())),
                    preferred_element_type=F32,
                )
                for x, first in ((gat, 0), (rou, TOP))
            )
            out[i * rows : (i + 1) * rows, feat:] = more.astype(BF)

    shape = (len(parts) * rows, feat + LANES)
    vmem = pl.BlockSpec(memory_space=pltpu.VMEM)
    return pl.pallas_call(
        body,
        name="join",
        out_shape=jax.ShapeDtypeStruct(shape, BF),
        in_specs=[vmem] * (3 * len(parts)),
        out_specs=vmem,
        cost_estimate=pl.CostEstimate(
            flops=0, bytes_accessed=4 * shape[0] * shape[1], transcendentals=0
        ),
    )(*[x for part in parts for x in part])


def experts(rows, target, w_in, w_out, feat):
    inner = w_out.shape[0]
    act = rows[:, :feat]
    gat = rows[:, feat : feat + TOP].astype(F32)
    rou = rows[:, feat + TOP : feat + 2 * TOP].astype(jnp.int32)
    share = jnp.sum(jnp.where(rou == target, gat, 0.0), axis=-1, keepdims=True)
    joined = jnp.dot(act, w_in, preferred_element_type=F32)
    hidden = (jax.nn.silu(joined[:, :inner]) * joined[:, inner:]).astype(BF)
    return jnp.dot(hidden, w_out, preferred_element_type=F32) * share


def a2a(x):
    return lax.all_to_all(x, "ep", split_axis=0, concat_axis=0, tiled=True)


def tiles(piece, pieces, unit, inner, columns):
    per_column = inner // unit
    for j in range(2 * inner // LANES):
        u = j * pieces + piece
        row = pl.multiple_of((u % per_column) * unit, unit)
        column = pl.multiple_of((u // per_column) * LANES, LANES)
        yield row, column, j * LANES


def pack(w_in, w_out, gi, part_rows, pieces):
    inner = w_out.shape[0]
    cut = part_rows // pieces
    unit = cut // 2
    step = 4

    def body(_, gate_ref, down_ref, out_ref):
        at = pl.program_id(0) * step
        for i in range(step):
            out_ref[i, :cut, :] = gate_ref[i * cut : (i + 1) * cut, :]
            for row, column, to in tiles(at + i, pieces, unit, inner, part_rows):
                out_ref[i, cut:, to : to + LANES] = down_ref[pl.ds(row, unit), pl.ds(column, LANES)]

    return pl.pallas_call(
        body,
        name="pack",
        out_shape=jax.ShapeDtypeStruct((pieces, cut + unit, 2 * inner), BF),
        grid_spec=pltpu.PrefetchScalarGridSpec(
            num_scalar_prefetch=1,
            grid=(pieces // step,),
            in_specs=[
                pl.BlockSpec((step * cut, 2 * inner), lambda p, g: (g[0] * (pieces // step) + p, 0)),
                pl.BlockSpec((inner, part_rows), lambda p, g: (0, g[0])),
            ],
            out_specs=pl.BlockSpec((step, cut + unit, 2 * inner), lambda p, g: (p, 0, 0)),
        ),
        compiler_params=pltpu.CompilerParams(vmem_limit_bytes=32 * 1024 * 1024),
        cost_estimate=pl.CostEstimate(
            flops=0, bytes_accessed=12 * part_rows * inner, transcendentals=0
        ),
    )(gi.reshape(1), w_in, w_out)


def unpack(packed, part_rows, inner):
    pieces = packed.shape[0]
    cut = part_rows // pieces
    unit = cut // 2
    step = 4

    def body(in_ref, gate_ref, down_ref):
        at = pl.program_id(0) * step
        for i in range(step):
            gate_ref[i * cut : (i + 1) * cut, :] = in_ref[i, :cut, :]
            for row, column, to in tiles(at + i, pieces, unit, inner, part_rows):
                down_ref[pl.ds(row, unit), pl.ds(column, LANES)] = in_ref[i, cut:, to : to + LANES]

    return pl.pallas_call(
        body,
        name="unpack",
        out_shape=[
            jax.ShapeDtypeStruct((part_rows, 2 * inner), BF),
            jax.ShapeDtypeStruct((inner, part_rows), BF),
        ],
        grid=(pieces // step,),
        in_specs=[pl.BlockSpec((step, cut + unit, 2 * inner), lambda p: (p, 0, 0))],
        out_specs=[
            pl.BlockSpec((step * cut, 2 * inner), lambda p: (p, 0)),
            pl.BlockSpec((inner, part_rows), lambda p: (0, 0)),
        ],
        compiler_params=pltpu.CompilerParams(vmem_limit_bytes=32 * 1024 * 1024),
        cost_estimate=pl.CostEstimate(
            flops=0, bytes_accessed=12 * part_rows * inner, transcendentals=0
        ),
    )(packed)


def local(
    tokens_one,
    routes_one,
    gates_one,
    tokens_two,
    routes_two,
    gates_two,
    old_table,
    new_table,
    gate_up,
    down_proj,
    norm_gain,
    kv_weight,
):
    w_in = gate_up[0]
    w_out = down_proj[0]
    ep = lax.axis_size("ep")
    grp = lax.axis_size("grp")
    me = lax.axis_index("ep")
    gi = lax.axis_index("grp")
    rows = tokens_one.shape[0]
    feat = w_in.shape[0]
    inner = w_out.shape[0]
    numbers = jnp.arange(ep, dtype=jnp.int32)
    sources_new = jnp.sum(
        (new_table[:, None] == old_table[None, :]).astype(jnp.int32) * numbers[None, :], axis=1
    )
    new_here = jnp.sum((sources_new == me).astype(jnp.int32) * numbers)

    mine = join(
        [(tokens_one, gates_one.T, routes_one.T), (tokens_two, gates_two.T, routes_two.T)]
    )
    far = [4 * i for i in range(1, ep // 4)]
    blocks = [mine] + [swap(mine, "ep", d) for d in far]

    part_rows = feat // grp
    cut = part_rows // ep
    packing = cut % 32 == 0 and inner % (cut // 2) == 0 and part_rows % LANES == 0 == inner % 64
    if packing:
        pieces = [pack(w_in, w_out, gi, part_rows, ep)]
    else:
        half_in = lax.dynamic_slice_in_dim(w_in, gi * part_rows, part_rows, 0)
        half_out = lax.dynamic_slice_in_dim(w_out, gi * part_rows, part_rows, 1)
        pieces = [half_in.reshape(ep, cut, 2 * inner), half_out.reshape(ep, inner // ep, part_rows)]
    near, pieces = lax.optimization_barrier((blocks[1], pieces))
    spread = [a2a(x) for x in pieces]
    line = jnp.concatenate([mine, near] + blocks[2:], axis=0)

    kv_blocks = [lax.optimization_barrier((kv_weight, line))[0]]
    for bit in range(grp.bit_length() - 1):
        kv_blocks = kv_blocks + [swap(x, "grp", 1 << bit) for x in kv_blocks]

    here = jnp.concatenate([line, swap(line, "ep", 2)], axis=0)
    there = swap(here, "ep", 1)
    target = jnp.concatenate([jnp.full((rows, 1), me), jnp.full((rows, 1), new_here)], axis=0)
    target = jnp.tile(target, (ep // 2, 1))
    kept = experts(here, target, w_in, w_out, feat)
    given = experts(there, target, w_in, w_out, feat).astype(BF)

    kept = kept + swap(given, "ep", 1).astype(F32)
    kept, wanted = lax.optimization_barrier((kept, sources_new))
    middle = kept.shape[0] // 2
    kept = kept[:middle] + swap(kept[middle:].astype(BF), "ep", 2).astype(F32)
    block = 2 * rows
    mix = kept[:block]
    for i, d in enumerate(far):
        mix = mix + swap(kept[(i + 1) * block : (i + 2) * block].astype(BF), "ep", d).astype(F32)
    own = jnp.concatenate([tokens_one, tokens_two], axis=0)
    hidden_all = (own.astype(F32) + mix).astype(BF)

    moved = [a2a(x[wanted]) for x in spread]
    if packing:
        gate_up_new, down_proj_new = unpack(moved[0], part_rows, inner)
    else:
        gate_up_new = moved[0].reshape(part_rows, 2 * inner)
        down_proj_new = moved[1].reshape(inner, part_rows)

    normed = rms_norm(hidden_all, norm_gain)
    blocks = [jnp.dot(normed, w, preferred_element_type=F32).astype(BF) for w in kv_blocks]
    kv = jnp.take(jnp.stack(blocks), gi ^ jnp.arange(grp), axis=0)
    kv = kv.transpose(1, 0, 2).reshape(2 * rows, -1)
    return (
        hidden_all[:rows],
        kv[:rows],
        hidden_all[rows:],
        kv[rows:],
        gate_up_new[None],
        down_proj_new[None],
    )


def solution(mesh):
    tok = P(("grp", "ep"), None)
    return jax.shard_map(
        local,
        mesh=mesh,
        in_specs=(
            tok,
            tok,
            tok,
            tok,
            tok,
            tok,
            P(),
            P(),
            P("ep", None, None),
            P("ep", None, None),
            P(),
            P(None, "grp"),
        ),
        out_specs=(tok, tok, tok, tok, P("ep", "grp", None), P("ep", None, "grp")),
        check_vma=False,
    )
```

```python
import jax
import jax.numpy as jnp
from jax import lax
from jax.experimental import pallas as pl
from jax.experimental.pallas import tpu as pltpu
from jax.sharding import PartitionSpec as P

TOP = 6
LANES = 128
BF = jnp.bfloat16
F32 = jnp.float32


def rms_norm(hidden, norm_gain):
    def body(hidden_ref, gain_ref, out_ref):
        values = hidden_ref[...].astype(F32)
        inverse_rms = lax.rsqrt(jnp.mean(values * values, axis=-1, keepdims=True) + 1e-06)
        out_ref[...] = (values * inverse_rms * gain_ref[...].astype(F32)).astype(BF)

    vmem = pl.BlockSpec(memory_space=pltpu.VMEM)
    return pl.pallas_call(
        body,
        name="rms_norm",
        out_shape=jax.ShapeDtypeStruct(hidden.shape, BF),
        in_specs=[vmem, vmem],
        out_specs=vmem,
        cost_estimate=pl.CostEstimate(flops=0, bytes_accessed=74_000_000, transcendentals=0),
    )(hidden, norm_gain.reshape(1, -1))


def swap(x, axis, distance):
    size = lax.axis_size(axis)
    return lax.ppermute(x, axis, [(i, i ^ distance) for i in range(size)])


def join(parts):
    rows, feat = parts[0][0].shape

    def body(*refs):
        out = refs[-1]
        for i in range(len(parts)):
            tok, gat, rou = refs[3 * i : 3 * i + 3]
            out[i * rows : (i + 1) * rows, :feat] = tok[...]
            lane = lax.broadcasted_iota(jnp.int32, (TOP, LANES), 1)
            line = lax.broadcasted_iota(jnp.int32, (TOP, LANES), 0)
            more = sum(
                lax.dot_general(
                    x[...].astype(F32).astype(BF),
                    (lane == line + first).astype(F32).astype(BF),
                    (((0,), (0,)), ((), ())),
                    preferred_element_type=F32,
                )
                for x, first in ((gat, 0), (rou, TOP))
            )
            out[i * rows : (i + 1) * rows, feat:] = more.astype(BF)

    shape = (len(parts) * rows, feat + LANES)
    vmem = pl.BlockSpec(memory_space=pltpu.VMEM)
    return pl.pallas_call(
        body,
        name="join",
        out_shape=jax.ShapeDtypeStruct(shape, BF),
        in_specs=[vmem] * (3 * len(parts)),
        out_specs=vmem,
        cost_estimate=pl.CostEstimate(
            flops=0, bytes_accessed=4 * shape[0] * shape[1], transcendentals=0
        ),
    )(*[x for part in parts for x in part])


def experts(rows, each, targets, w_in, w_out, dtype):
    inner, feat = w_out.shape
    count = rows.shape[0]
    width = rows.shape[1]
    step = min(256, count)

    def body(target_ref, row_ref, in_ref, out_w_ref, out_ref):
        joined = jnp.dot(row_ref[:, :feat], in_ref[...], preferred_element_type=F32)
        upward = pltpu.roll(joined, inner, 1)
        hidden = joined / (1.0 + jnp.exp(-joined)) * upward
        hidden = hidden[:, :inner].astype(BF)
        result = jnp.dot(hidden, out_w_ref[...], preferred_element_type=F32)
        more = row_ref[:, feat:].astype(F32)
        routes = pltpu.roll(more, LANES - TOP, 1)
        lane = lax.broadcasted_iota(jnp.int32, more.shape, 1)
        line = lax.broadcasted_iota(jnp.int32, more.shape, 0)
        target = jnp.where(line % (2 * each) < each, target_ref[0], target_ref[1]).astype(F32)
        chosen = (routes == target) & (lane < TOP)
        share = jnp.sum(jnp.where(chosen, more, 0.0), axis=1, keepdims=True)
        out_ref[...] = (result * share).astype(dtype)

    return pl.pallas_call(
        body,
        name="experts",
        out_shape=jax.ShapeDtypeStruct((count, feat), dtype),
        grid=(count // step,),
        in_specs=[
            pl.BlockSpec(memory_space=pltpu.SMEM),
            pl.BlockSpec((step, width), lambda i: (i, 0)),
            pl.BlockSpec(w_in.shape, lambda i: (0, 0)),
            pl.BlockSpec(w_out.shape, lambda i: (0, 0)),
        ],
        out_specs=pl.BlockSpec((step, feat), lambda i: (i, 0)),
        compiler_params=pltpu.CompilerParams(vmem_limit_bytes=48 * 1024 * 1024),
        cost_estimate=pl.CostEstimate(flops=0, bytes_accessed=0, transcendentals=0),
    )(targets, rows, w_in, w_out)


def a2a(x):
    return lax.all_to_all(x, "ep", split_axis=0, concat_axis=0, tiled=True)


def tiles(piece, pieces, unit, inner, columns):
    per_column = inner // unit
    for j in range(2 * inner // LANES):
        u = j * pieces + piece
        row = pl.multiple_of((u % per_column) * unit, unit)
        column = pl.multiple_of((u // per_column) * LANES, LANES)
        yield row, column, j * LANES


def pack(w_in, w_out, gi, part_rows, pieces):
    inner = w_out.shape[0]
    cut = part_rows // pieces
    unit = cut // 2
    step = 4

    def body(_, gate_ref, down_ref, out_ref):
        at = pl.program_id(0) * step
        for i in range(step):
            out_ref[i, :cut, :] = gate_ref[i * cut : (i + 1) * cut, :]
            for row, column, to in tiles(at + i, pieces, unit, inner, part_rows):
                out_ref[i, cut:, to : to + LANES] = down_ref[pl.ds(row, unit), pl.ds(column, LANES)]

    return pl.pallas_call(
        body,
        name="pack",
        out_shape=jax.ShapeDtypeStruct((pieces, cut + unit, 2 * inner), BF),
        grid_spec=pltpu.PrefetchScalarGridSpec(
            num_scalar_prefetch=1,
            grid=(pieces // step,),
            in_specs=[
                pl.BlockSpec((step * cut, 2 * inner), lambda p, g: (g[0] * (pieces // step) + p, 0)),
                pl.BlockSpec((inner, part_rows), lambda p, g: (0, g[0])),
            ],
            out_specs=pl.BlockSpec((step, cut + unit, 2 * inner), lambda p, g: (p, 0, 0)),
        ),
        compiler_params=pltpu.CompilerParams(vmem_limit_bytes=32 * 1024 * 1024),
        cost_estimate=pl.CostEstimate(
            flops=0, bytes_accessed=12 * part_rows * inner, transcendentals=0
        ),
    )(gi.reshape(1), w_in, w_out)


def unpack(packed, part_rows, inner):
    pieces = packed.shape[0]
    cut = part_rows // pieces
    unit = cut // 2
    step = 4

    def body(in_ref, gate_ref, down_ref):
        at = pl.program_id(0) * step
        for i in range(step):
            gate_ref[i * cut : (i + 1) * cut, :] = in_ref[i, :cut, :]
            for row, column, to in tiles(at + i, pieces, unit, inner, part_rows):
                down_ref[pl.ds(row, unit), pl.ds(column, LANES)] = in_ref[i, cut:, to : to + LANES]

    return pl.pallas_call(
        body,
        name="unpack",
        out_shape=[
            jax.ShapeDtypeStruct((part_rows, 2 * inner), BF),
            jax.ShapeDtypeStruct((inner, part_rows), BF),
        ],
        grid=(pieces // step,),
        in_specs=[pl.BlockSpec((step, cut + unit, 2 * inner), lambda p: (p, 0, 0))],
        out_specs=[
            pl.BlockSpec((step * cut, 2 * inner), lambda p: (p, 0)),
            pl.BlockSpec((inner, part_rows), lambda p: (0, 0)),
        ],
        compiler_params=pltpu.CompilerParams(vmem_limit_bytes=32 * 1024 * 1024),
        cost_estimate=pl.CostEstimate(
            flops=0, bytes_accessed=12 * part_rows * inner, transcendentals=0
        ),
    )(packed)


def local(
    tokens_one,
    routes_one,
    gates_one,
    tokens_two,
    routes_two,
    gates_two,
    old_table,
    new_table,
    gate_up,
    down_proj,
    norm_gain,
    kv_weight,
):
    w_in = gate_up[0]
    w_out = down_proj[0]
    ep = lax.axis_size("ep")
    grp = lax.axis_size("grp")
    me = lax.axis_index("ep")
    gi = lax.axis_index("grp")
    rows = tokens_one.shape[0]
    feat = w_in.shape[0]
    inner = w_out.shape[0]
    numbers = jnp.arange(ep, dtype=jnp.int32)
    sources_new = jnp.sum(
        (new_table[:, None] == old_table[None, :]).astype(jnp.int32) * numbers[None, :], axis=1
    )
    new_here = jnp.sum((sources_new == me).astype(jnp.int32) * numbers)

    mine = join(
        [(tokens_one, gates_one.T, routes_one.T), (tokens_two, gates_two.T, routes_two.T)]
    )
    far = [4 * i for i in range(1, ep // 4)]
    blocks = [mine] + [swap(mine, "ep", d) for d in far]

    part_rows = feat // grp
    cut = part_rows // ep
    packing = cut % 32 == 0 and inner % (cut // 2) == 0 and part_rows % LANES == 0 == inner % 64
    if packing:
        pieces = [pack(w_in, w_out, gi, part_rows, ep)]
    else:
        half_in = lax.dynamic_slice_in_dim(w_in, gi * part_rows, part_rows, 0)
        half_out = lax.dynamic_slice_in_dim(w_out, gi * part_rows, part_rows, 1)
        pieces = [half_in.reshape(ep, cut, 2 * inner), half_out.reshape(ep, inner // ep, part_rows)]
    near, pieces = lax.optimization_barrier((blocks[1], pieces))
    spread = [a2a(x) for x in pieces]
    line = jnp.concatenate([mine, near] + blocks[2:], axis=0)

    kv_blocks = [lax.optimization_barrier((kv_weight, line))[0]]
    for bit in range(grp.bit_length() - 1):
        kv_blocks = kv_blocks + [swap(x, "grp", 1 << bit) for x in kv_blocks]

    here = jnp.concatenate([line, swap(line, "ep", 2)], axis=0)
    there = swap(here, "ep", 1)
    targets = jnp.stack([me, new_here])
    kept = experts(here, rows, targets, w_in, w_out, F32)
    given = experts(there, rows, targets, w_in, w_out, BF)

    kept = kept + swap(given, "ep", 1).astype(F32)
    kept, wanted = lax.optimization_barrier((kept, sources_new))
    moved = [a2a(x[wanted]) for x in spread]
    middle = kept.shape[0] // 2
    kept = kept[:middle] + swap(kept[middle:].astype(BF), "ep", 2).astype(F32)
    block = 2 * rows
    mix = kept[:block]
    for i, d in enumerate(far):
        mix = mix + swap(kept[(i + 1) * block : (i + 2) * block].astype(BF), "ep", d).astype(F32)
    own = jnp.concatenate([tokens_one, tokens_two], axis=0)
    hidden_all = (own.astype(F32) + mix).astype(BF)

    if packing:
        gate_up_new, down_proj_new = unpack(moved[0], part_rows, inner)
    else:
        gate_up_new = moved[0].reshape(part_rows, 2 * inner)
        down_proj_new = moved[1].reshape(inner, part_rows)

    normed = rms_norm(hidden_all, norm_gain)
    blocks = [jnp.dot(normed, w, preferred_element_type=F32).astype(BF) for w in kv_blocks]
    kv = jnp.take(jnp.stack(blocks), gi ^ jnp.arange(grp), axis=0)
    kv = kv.transpose(1, 0, 2).reshape(2 * rows, -1)
    return (
        hidden_all[:rows],
        kv[:rows],
        hidden_all[rows:],
        kv[rows:],
        gate_up_new[None],
        down_proj_new[None],
    )


def solution(mesh):
    tok = P(("grp", "ep"), None)
    return jax.shard_map(
        local,
        mesh=mesh,
        in_specs=(
            tok,
            tok,
            tok,
            tok,
            tok,
            tok,
            P(),
            P(),
            P("ep", None, None),
            P("ep", None, None),
            P(),
            P(None, "grp"),
        ),
        out_specs=(tok, tok, tok, tok, P("ep", "grp", None), P("ep", None, "grp")),
        check_vma=False,
    )
```

```python
import jax
import jax.numpy as jnp
from jax import lax
from jax.experimental import pallas as pl
from jax.experimental.pallas import tpu as pltpu
from jax.sharding import PartitionSpec as P

TOP = 6
LANES = 128
BF = jnp.bfloat16
F32 = jnp.float32


def rms_norm(hidden, norm_gain):
    values = hidden.astype(F32)
    inverse_rms = lax.rsqrt(jnp.mean(values * values, axis=-1, keepdims=True) + 1e-06)
    return (values * inverse_rms * norm_gain.astype(F32)).astype(BF)


def swap(x, axis, distance):
    size = lax.axis_size(axis)
    return lax.ppermute(x, axis, [(i, i ^ distance) for i in range(size)])


def join(parts):
    rows, feat = parts[0][0].shape

    def body(*refs):
        out = refs[-1]
        for i in range(len(parts)):
            tok, gat, rou = refs[3 * i : 3 * i + 3]
            out[i * rows : (i + 1) * rows, :feat] = tok[...]
            lane = lax.broadcasted_iota(jnp.int32, (TOP, LANES), 1)
            line = lax.broadcasted_iota(jnp.int32, (TOP, LANES), 0)
            more = sum(
                lax.dot_general(
                    x[...].astype(F32).astype(BF),
                    (lane == line + first).astype(F32).astype(BF),
                    (((0,), (0,)), ((), ())),
                    preferred_element_type=F32,
                )
                for x, first in ((gat, 0), (rou, TOP))
            )
            out[i * rows : (i + 1) * rows, feat:] = more.astype(BF)

    shape = (len(parts) * rows, feat + LANES)
    vmem = pl.BlockSpec(memory_space=pltpu.VMEM)
    return pl.pallas_call(
        body,
        name="join",
        out_shape=jax.ShapeDtypeStruct(shape, BF),
        in_specs=[vmem] * (3 * len(parts)),
        out_specs=vmem,
        cost_estimate=pl.CostEstimate(
            flops=0, bytes_accessed=4 * shape[0] * shape[1], transcendentals=0
        ),
    )(*[x for part in parts for x in part])


def experts(rows, each, targets, w_in, w_out, dtype):
    inner, feat = w_out.shape
    count = rows.shape[0]
    width = rows.shape[1]
    step = min(256, count)

    def body(target_ref, row_ref, in_ref, out_w_ref, out_ref):
        joined = jnp.dot(row_ref[:, :feat], in_ref[...], preferred_element_type=F32)
        upward = pltpu.roll(joined, inner, 1)
        hidden = joined / (1.0 + jnp.exp(-joined)) * upward
        hidden = hidden[:, :inner].astype(BF)
        result = jnp.dot(hidden, out_w_ref[...], preferred_element_type=F32)
        more = row_ref[:, feat:].astype(F32)
        routes = pltpu.roll(more, LANES - TOP, 1)
        lane = lax.broadcasted_iota(jnp.int32, more.shape, 1)
        line = lax.broadcasted_iota(jnp.int32, more.shape, 0)
        target = jnp.where(line % (2 * each) < each, target_ref[0], target_ref[1]).astype(F32)
        chosen = (routes == target) & (lane < TOP)
        share = jnp.sum(jnp.where(chosen, more, 0.0), axis=1, keepdims=True)
        out_ref[...] = (result * share).astype(dtype)

    return pl.pallas_call(
        body,
        name="experts",
        out_shape=jax.ShapeDtypeStruct((count, feat), dtype),
        grid=(count // step,),
        in_specs=[
            pl.BlockSpec(memory_space=pltpu.SMEM),
            pl.BlockSpec((step, width), lambda i: (i, 0)),
            pl.BlockSpec(w_in.shape, lambda i: (0, 0)),
            pl.BlockSpec(w_out.shape, lambda i: (0, 0)),
        ],
        out_specs=pl.BlockSpec((step, feat), lambda i: (i, 0)),
        compiler_params=pltpu.CompilerParams(vmem_limit_bytes=48 * 1024 * 1024),
        cost_estimate=pl.CostEstimate(flops=0, bytes_accessed=0, transcendentals=0),
    )(targets, rows, w_in, w_out)


def a2a(x):
    return lax.all_to_all(x, "ep", split_axis=0, concat_axis=0, tiled=True)


def tiles(piece, pieces, unit, inner, columns):
    per_column = inner // unit
    for j in range(2 * inner // LANES):
        u = j * pieces + piece
        row = pl.multiple_of((u % per_column) * unit, unit)
        column = pl.multiple_of((u // per_column) * LANES, LANES)
        yield row, column, j * LANES


def pack(w_in, w_out, gi, part_rows, pieces):
    inner = w_out.shape[0]
    cut = part_rows // pieces
    unit = cut // 2
    step = 4

    def body(_, gate_ref, down_ref, out_ref):
        at = pl.program_id(0) * step
        for i in range(step):
            out_ref[i, :cut, :] = gate_ref[i * cut : (i + 1) * cut, :]
            for row, column, to in tiles(at + i, pieces, unit, inner, part_rows):
                out_ref[i, cut:, to : to + LANES] = down_ref[pl.ds(row, unit), pl.ds(column, LANES)]

    return pl.pallas_call(
        body,
        name="pack",
        out_shape=jax.ShapeDtypeStruct((pieces, cut + unit, 2 * inner), BF),
        grid_spec=pltpu.PrefetchScalarGridSpec(
            num_scalar_prefetch=1,
            grid=(pieces // step,),
            in_specs=[
                pl.BlockSpec((step * cut, 2 * inner), lambda p, g: (g[0] * (pieces // step) + p, 0)),
                pl.BlockSpec((inner, part_rows), lambda p, g: (0, g[0])),
            ],
            out_specs=pl.BlockSpec((step, cut + unit, 2 * inner), lambda p, g: (p, 0, 0)),
        ),
        compiler_params=pltpu.CompilerParams(vmem_limit_bytes=32 * 1024 * 1024),
        cost_estimate=pl.CostEstimate(
            flops=0, bytes_accessed=12 * part_rows * inner, transcendentals=0
        ),
    )(gi.reshape(1), w_in, w_out)


def unpack(packed, part_rows, inner):
    pieces = packed.shape[0]
    cut = part_rows // pieces
    unit = cut // 2
    step = 4

    def body(in_ref, gate_ref, down_ref):
        at = pl.program_id(0) * step
        for i in range(step):
            gate_ref[i * cut : (i + 1) * cut, :] = in_ref[i, :cut, :]
            for row, column, to in tiles(at + i, pieces, unit, inner, part_rows):
                down_ref[pl.ds(row, unit), pl.ds(column, LANES)] = in_ref[i, cut:, to : to + LANES]

    return pl.pallas_call(
        body,
        name="unpack",
        out_shape=[
            jax.ShapeDtypeStruct((part_rows, 2 * inner), BF),
            jax.ShapeDtypeStruct((inner, part_rows), BF),
        ],
        grid=(pieces // step,),
        in_specs=[pl.BlockSpec((step, cut + unit, 2 * inner), lambda p: (p, 0, 0))],
        out_specs=[
            pl.BlockSpec((step * cut, 2 * inner), lambda p: (p, 0)),
            pl.BlockSpec((inner, part_rows), lambda p: (0, 0)),
        ],
        compiler_params=pltpu.CompilerParams(vmem_limit_bytes=32 * 1024 * 1024),
        cost_estimate=pl.CostEstimate(
            flops=0, bytes_accessed=12 * part_rows * inner, transcendentals=0
        ),
    )(packed)


def local(
    tokens_one,
    routes_one,
    gates_one,
    tokens_two,
    routes_two,
    gates_two,
    old_table,
    new_table,
    gate_up,
    down_proj,
    norm_gain,
    kv_weight,
):
    w_in = gate_up[0]
    w_out = down_proj[0]
    ep = lax.axis_size("ep")
    grp = lax.axis_size("grp")
    me = lax.axis_index("ep")
    gi = lax.axis_index("grp")
    rows = tokens_one.shape[0]
    feat = w_in.shape[0]
    inner = w_out.shape[0]
    numbers = jnp.arange(ep, dtype=jnp.int32)
    sources_new = jnp.sum(
        (new_table[:, None] == old_table[None, :]).astype(jnp.int32) * numbers[None, :], axis=1
    )
    new_here = jnp.sum((sources_new == me).astype(jnp.int32) * numbers)

    mine = join(
        [(tokens_one, gates_one.T, routes_one.T), (tokens_two, gates_two.T, routes_two.T)]
    )
    far = [4 * i for i in range(1, ep // 4)]
    blocks = [mine] + [swap(mine, "ep", d) for d in far]

    part_rows = feat // grp
    cut = part_rows // ep
    packing = cut % 32 == 0 and inner % (cut // 2) == 0 and part_rows % LANES == 0 == inner % 64
    if packing:
        pieces = [pack(w_in, w_out, gi, part_rows, ep)]
    else:
        half_in = lax.dynamic_slice_in_dim(w_in, gi * part_rows, part_rows, 0)
        half_out = lax.dynamic_slice_in_dim(w_out, gi * part_rows, part_rows, 1)
        pieces = [half_in.reshape(ep, cut, 2 * inner), half_out.reshape(ep, inner // ep, part_rows)]
    blocks, pieces = lax.optimization_barrier((blocks, pieces))
    spread = [a2a(x) for x in pieces]
    line = jnp.concatenate(blocks, axis=0)

    kv_blocks = [lax.optimization_barrier((kv_weight, line))[0]]
    for bit in range(grp.bit_length() - 1):
        kv_blocks = kv_blocks + [swap(x, "grp", 1 << bit) for x in kv_blocks]

    here = jnp.concatenate([line, swap(line, "ep", 2)], axis=0)
    there = swap(here, "ep", 1)
    targets = jnp.stack([me, new_here])
    kept = experts(here, rows, targets, w_in, w_out, F32)
    given = experts(there, rows, targets, w_in, w_out, BF)

    kept = kept + swap(given, "ep", 1).astype(F32)
    middle = kept.shape[0] // 2
    sent, wanted = lax.optimization_barrier((kept[middle:].astype(BF), sources_new))
    kept = kept[:middle] + swap(sent, "ep", 2).astype(F32)
    kept, wanted = lax.optimization_barrier((kept, wanted))
    moved = [a2a(x[wanted]) for x in spread]
    planes = jnp.arange(ep // 4, dtype=jnp.int32)
    parts = kept.astype(BF).reshape(ep // 4, 2 * rows, feat)[planes ^ (me // 4)]
    mix = lax.psum_scatter(
        parts.reshape(-1, feat),
        "ep",
        scatter_dimension=0,
        axis_index_groups=[[r + 4 * i for i in range(ep // 4)] for r in range(4)],
        tiled=True,
    ).astype(F32)
    own = jnp.concatenate([tokens_one, tokens_two], axis=0)
    hidden_all = (own.astype(F32) + mix).astype(BF)

    if packing:
        gate_up_new, down_proj_new = unpack(moved[0], part_rows, inner)
    else:
        gate_up_new = moved[0].reshape(part_rows, 2 * inner)
        down_proj_new = moved[1].reshape(inner, part_rows)

    normed = rms_norm(hidden_all, norm_gain)
    blocks = [jnp.dot(normed, w, preferred_element_type=F32).astype(BF) for w in kv_blocks]
    kv = jnp.take(jnp.stack(blocks), gi ^ jnp.arange(grp), axis=0)
    kv = kv.transpose(1, 0, 2).reshape(2 * rows, -1)
    return (
        hidden_all[:rows],
        kv[:rows],
        hidden_all[rows:],
        kv[rows:],
        gate_up_new[None],
        down_proj_new[None],
    )


def solution(mesh):
    tok = P(("grp", "ep"), None)
    return jax.shard_map(
        local,
        mesh=mesh,
        in_specs=(
            tok,
            tok,
            tok,
            tok,
            tok,
            tok,
            P(),
            P(),
            P("ep", None, None),
            P("ep", None, None),
            P(),
            P(None, "grp"),
        ),
        out_specs=(tok, tok, tok, tok, P("ep", "grp", None), P("ep", None, "grp")),
        check_vma=False,
    )
```

```python
import jax
import jax.numpy as jnp
from jax import lax
from jax.experimental import pallas as pl
from jax.experimental.pallas import tpu as pltpu
from jax.sharding import PartitionSpec as P

TOP = 6
LANES = 128
BF = jnp.bfloat16
F32 = jnp.float32


def rms_norm(hidden, norm_gain):
    values = hidden.astype(F32)
    inverse_rms = lax.rsqrt(jnp.mean(values * values, axis=-1, keepdims=True) + 1e-06)
    return (values * inverse_rms * norm_gain.astype(F32)).astype(BF)


def swap(x, axis, distance):
    size = lax.axis_size(axis)
    return lax.ppermute(x, axis, [(i, i ^ distance) for i in range(size)])


def join(parts):
    rows, feat = parts[0][0].shape

    def body(*refs):
        out = refs[-1]
        for i in range(len(parts)):
            tok, gat, rou = refs[3 * i : 3 * i + 3]
            out[i * rows : (i + 1) * rows, :feat] = tok[...]
            lane = lax.broadcasted_iota(jnp.int32, (TOP, LANES), 1)
            line = lax.broadcasted_iota(jnp.int32, (TOP, LANES), 0)
            more = sum(
                lax.dot_general(
                    x[...].astype(F32).astype(BF),
                    (lane == line + first).astype(F32).astype(BF),
                    (((0,), (0,)), ((), ())),
                    preferred_element_type=F32,
                )
                for x, first in ((gat, 0), (rou, TOP))
            )
            out[i * rows : (i + 1) * rows, feat:] = more.astype(BF)

    shape = (len(parts) * rows, feat + LANES)
    vmem = pl.BlockSpec(memory_space=pltpu.VMEM)
    return pl.pallas_call(
        body,
        name="join",
        out_shape=jax.ShapeDtypeStruct(shape, BF),
        in_specs=[vmem] * (3 * len(parts)),
        out_specs=vmem,
        cost_estimate=pl.CostEstimate(
            flops=0, bytes_accessed=4 * shape[0] * shape[1], transcendentals=0
        ),
    )(*[x for part in parts for x in part])


def experts(here, there, half, each, targets, w_in, w_out):
    inner, feat = w_out.shape
    count = here.shape[0] // 2
    width = here.shape[1]
    step = min(256, count)

    def body(target_ref, here_ref, there_ref, in_ref, out_w_ref, kept_ref, given_ref):
        for row_ref, out_ref in ((there_ref, given_ref), (here_ref, kept_ref)):
            joined = jnp.dot(row_ref[:, :feat], in_ref[...], preferred_element_type=F32)
            upward = pltpu.roll(joined, inner, 1)
            hidden = joined / (1.0 + jnp.exp(-joined)) * upward
            hidden = hidden[:, :inner].astype(BF)
            result = jnp.dot(hidden, out_w_ref[...], preferred_element_type=F32)
            more = row_ref[:, feat:].astype(F32)
            routes = pltpu.roll(more, LANES - TOP, 1)
            lane = lax.broadcasted_iota(jnp.int32, more.shape, 1)
            line = lax.broadcasted_iota(jnp.int32, more.shape, 0)
            target = jnp.where(line % (2 * each) < each, target_ref[0], target_ref[1])
            chosen = (routes == target.astype(F32)) & (lane < TOP)
            share = jnp.sum(jnp.where(chosen, more, 0.0), axis=1, keepdims=True)
            out_ref[...] = (result * share).astype(out_ref.dtype)

    first = half * (count // step)
    return pl.pallas_call(
        body,
        name="experts",
        out_shape=[
            jax.ShapeDtypeStruct((count, feat), F32),
            jax.ShapeDtypeStruct((count, feat), BF),
        ],
        grid=(count // step,),
        in_specs=[
            pl.BlockSpec(memory_space=pltpu.SMEM),
            pl.BlockSpec((step, width), lambda i: (first + i, 0)),
            pl.BlockSpec((step, width), lambda i: (first + i, 0)),
            pl.BlockSpec(w_in.shape, lambda i: (0, 0)),
            pl.BlockSpec(w_out.shape, lambda i: (0, 0)),
        ],
        out_specs=[pl.BlockSpec((step, feat), lambda i: (i, 0))] * 2,
        compiler_params=pltpu.CompilerParams(vmem_limit_bytes=48 * 1024 * 1024),
        cost_estimate=pl.CostEstimate(flops=0, bytes_accessed=0, transcendentals=0),
    )(targets, here, there, w_in, w_out)


def a2a(x):
    return lax.all_to_all(x, "ep", split_axis=0, concat_axis=0, tiled=True)


def tiles(piece, pieces, unit, inner, columns):
    per_column = inner // unit
    for j in range(2 * inner // LANES):
        u = j * pieces + piece
        row = pl.multiple_of((u % per_column) * unit, unit)
        column = pl.multiple_of((u // per_column) * LANES, LANES)
        yield row, column, j * LANES


def pack(w_in, w_out, gi, part_rows, pieces):
    inner = w_out.shape[0]
    cut = part_rows // pieces
    unit = cut // 2
    step = 4

    def body(_, gate_ref, down_ref, out_ref):
        at = pl.program_id(0) * step
        for i in range(step):
            out_ref[i, :cut, :] = gate_ref[i * cut : (i + 1) * cut, :]
            for row, column, to in tiles(at + i, pieces, unit, inner, part_rows):
                out_ref[i, cut:, to : to + LANES] = down_ref[pl.ds(row, unit), pl.ds(column, LANES)]

    return pl.pallas_call(
        body,
        name="pack",
        out_shape=jax.ShapeDtypeStruct((pieces, cut + unit, 2 * inner), BF),
        grid_spec=pltpu.PrefetchScalarGridSpec(
            num_scalar_prefetch=1,
            grid=(pieces // step,),
            in_specs=[
                pl.BlockSpec((step * cut, 2 * inner), lambda p, g: (g[0] * (pieces // step) + p, 0)),
                pl.BlockSpec((inner, part_rows), lambda p, g: (0, g[0])),
            ],
            out_specs=pl.BlockSpec((step, cut + unit, 2 * inner), lambda p, g: (p, 0, 0)),
        ),
        compiler_params=pltpu.CompilerParams(vmem_limit_bytes=32 * 1024 * 1024),
        cost_estimate=pl.CostEstimate(
            flops=0, bytes_accessed=12 * part_rows * inner, transcendentals=0
        ),
    )(gi.reshape(1), w_in, w_out)


def unpack(packed, part_rows, inner):
    pieces = packed.shape[0]
    cut = part_rows // pieces
    unit = cut // 2
    step = 4

    def body(in_ref, gate_ref, down_ref):
        at = pl.program_id(0) * step
        for i in range(step):
            gate_ref[i * cut : (i + 1) * cut, :] = in_ref[i, :cut, :]
            for row, column, to in tiles(at + i, pieces, unit, inner, part_rows):
                down_ref[pl.ds(row, unit), pl.ds(column, LANES)] = in_ref[i, cut:, to : to + LANES]

    return pl.pallas_call(
        body,
        name="unpack",
        out_shape=[
            jax.ShapeDtypeStruct((part_rows, 2 * inner), BF),
            jax.ShapeDtypeStruct((inner, part_rows), BF),
        ],
        grid=(pieces // step,),
        in_specs=[pl.BlockSpec((step, cut + unit, 2 * inner), lambda p: (p, 0, 0))],
        out_specs=[
            pl.BlockSpec((step * cut, 2 * inner), lambda p: (p, 0)),
            pl.BlockSpec((inner, part_rows), lambda p: (0, 0)),
        ],
        compiler_params=pltpu.CompilerParams(vmem_limit_bytes=32 * 1024 * 1024),
        cost_estimate=pl.CostEstimate(
            flops=0, bytes_accessed=12 * part_rows * inner, transcendentals=0
        ),
    )(packed)


def local(
    tokens_one,
    routes_one,
    gates_one,
    tokens_two,
    routes_two,
    gates_two,
    old_table,
    new_table,
    gate_up,
    down_proj,
    norm_gain,
    kv_weight,
):
    w_in = gate_up[0]
    w_out = down_proj[0]
    ep = lax.axis_size("ep")
    grp = lax.axis_size("grp")
    me = lax.axis_index("ep")
    gi = lax.axis_index("grp")
    rows = tokens_one.shape[0]
    feat = w_in.shape[0]
    inner = w_out.shape[0]
    numbers = jnp.arange(ep, dtype=jnp.int32)
    sources_new = jnp.sum(
        (new_table[:, None] == old_table[None, :]).astype(jnp.int32) * numbers[None, :], axis=1
    )
    new_here = jnp.sum((sources_new == me).astype(jnp.int32) * numbers)

    mine = join(
        [(tokens_one, gates_one.T, routes_one.T), (tokens_two, gates_two.T, routes_two.T)]
    )
    far = [4 * i for i in range(1, ep // 4)]
    blocks = [mine] + [swap(mine, "ep", d) for d in far]

    part_rows = feat // grp
    cut = part_rows // ep
    packing = cut % 32 == 0 and inner % (cut // 2) == 0 and part_rows % LANES == 0 == inner % 64
    if packing:
        pieces = [pack(w_in, w_out, gi, part_rows, ep)]
    else:
        half_in = lax.dynamic_slice_in_dim(w_in, gi * part_rows, part_rows, 0)
        half_out = lax.dynamic_slice_in_dim(w_out, gi * part_rows, part_rows, 1)
        pieces = [half_in.reshape(ep, cut, 2 * inner), half_out.reshape(ep, inner // ep, part_rows)]
    near, pieces = lax.optimization_barrier((blocks[1], pieces))
    spread = [a2a(x) for x in pieces]
    line = jnp.concatenate([mine, near] + blocks[2:], axis=0)

    kv_blocks = [lax.optimization_barrier((kv_weight, line))[0]]
    for bit in range(grp.bit_length() - 1):
        kv_blocks = kv_blocks + [swap(x, "grp", 1 << bit) for x in kv_blocks]

    here = jnp.concatenate([line, swap(line, "ep", 2)], axis=0)
    there = swap(here, "ep", 1)
    targets = jnp.stack([me, new_here])

    kept, given = experts(here, there, 1, rows, targets, w_in, w_out)
    sent = (kept + swap(given, "ep", 1).astype(F32)).astype(BF)
    sent, here, wanted = lax.optimization_barrier((sent, here, sources_new))
    came = swap(sent, "ep", 2)
    kept, given = experts(here, there, 0, rows, targets, w_in, w_out)
    kept = kept + swap(given, "ep", 1).astype(F32) + came.astype(F32)
    kept, wanted = lax.optimization_barrier((kept, wanted))
    block = 2 * rows
    sent = [kept[(i + 1) * block : (i + 2) * block].astype(BF) for i in range(len(far))]
    came = [swap(x, "ep", d) for x, d in zip(sent, far)]
    grouped = [x[wanted] for x in spread]
    came, grouped = lax.optimization_barrier((came, grouped))
    moved = [a2a(x) for x in grouped]
    mix = kept[:block] + sum(x.astype(F32) for x in came)
    own = jnp.concatenate([tokens_one, tokens_two], axis=0)
    hidden_all = (own.astype(F32) + mix).astype(BF)

    if packing:
        gate_up_new, down_proj_new = unpack(moved[0], part_rows, inner)
    else:
        gate_up_new = moved[0].reshape(part_rows, 2 * inner)
        down_proj_new = moved[1].reshape(inner, part_rows)

    normed = rms_norm(hidden_all, norm_gain)
    blocks = [jnp.dot(normed, w, preferred_element_type=F32).astype(BF) for w in kv_blocks]
    kv = jnp.take(jnp.stack(blocks), gi ^ jnp.arange(grp), axis=0)
    kv = kv.transpose(1, 0, 2).reshape(2 * rows, -1)
    return (
        hidden_all[:rows],
        kv[:rows],
        hidden_all[rows:],
        kv[rows:],
        gate_up_new[None],
        down_proj_new[None],
    )


def solution(mesh):
    tok = P(("grp", "ep"), None)
    return jax.shard_map(
        local,
        mesh=mesh,
        in_specs=(
            tok,
            tok,
            tok,
            tok,
            tok,
            tok,
            P(),
            P(),
            P("ep", None, None),
            P("ep", None, None),
            P(),
            P(None, "grp"),
        ),
        out_specs=(tok, tok, tok, tok, P("ep", "grp", None), P("ep", None, "grp")),
        check_vma=False,
    )
```

```python
import jax
import jax.numpy as jnp
from jax import lax
from jax.experimental import pallas as pl
from jax.experimental.pallas import tpu as pltpu
from jax.sharding import PartitionSpec as P

TOP = 6
LANES = 128
BF = jnp.bfloat16
F32 = jnp.float32


def rms_norm(hidden, norm_gain):
    values = hidden.astype(F32)
    inverse_rms = lax.rsqrt(jnp.mean(values * values, axis=-1, keepdims=True) + 1e-06)
    return (values * inverse_rms * norm_gain.astype(F32)).astype(BF)


def swap(x, axis, distance):
    size = lax.axis_size(axis)
    return lax.ppermute(x, axis, [(i, i ^ distance) for i in range(size)])


def join(parts):
    rows, feat = parts[0][0].shape

    def body(*refs):
        out = refs[-1]
        for i in range(len(parts)):
            tok, gat, rou = refs[3 * i : 3 * i + 3]
            out[i * rows : (i + 1) * rows, :feat] = tok[...]
            lane = lax.broadcasted_iota(jnp.int32, (TOP, LANES), 1)
            line = lax.broadcasted_iota(jnp.int32, (TOP, LANES), 0)
            more = sum(
                lax.dot_general(
                    x[...].astype(F32).astype(BF),
                    (lane == line + first).astype(F32).astype(BF),
                    (((0,), (0,)), ((), ())),
                    preferred_element_type=F32,
                )
                for x, first in ((gat, 0), (rou, TOP))
            )
            out[i * rows : (i + 1) * rows, feat:] = more.astype(BF)

    shape = (len(parts) * rows, feat + LANES)
    vmem = pl.BlockSpec(memory_space=pltpu.VMEM)
    return pl.pallas_call(
        body,
        name="join",
        out_shape=jax.ShapeDtypeStruct(shape, BF),
        in_specs=[vmem] * (3 * len(parts)),
        out_specs=vmem,
        cost_estimate=pl.CostEstimate(
            flops=0, bytes_accessed=4 * shape[0] * shape[1], transcendentals=0
        ),
    )(*[x for part in parts for x in part])


def experts(here, there, half, each, targets, w_in, w_out):
    inner, feat = w_out.shape
    count = here.shape[0] // 2
    width = here.shape[1]
    step = min(256, count)

    def body(target_ref, here_ref, there_ref, in_ref, out_w_ref, kept_ref, given_ref):
        for row_ref, out_ref in ((there_ref, given_ref), (here_ref, kept_ref)):
            joined = jnp.dot(row_ref[:, :feat], in_ref[...], preferred_element_type=F32)
            upward = pltpu.roll(joined, inner, 1)
            hidden = joined / (1.0 + jnp.exp(-joined)) * upward
            hidden = hidden[:, :inner].astype(BF)
            result = jnp.dot(hidden, out_w_ref[...], preferred_element_type=F32)
            more = row_ref[:, feat:].astype(F32)
            routes = pltpu.roll(more, LANES - TOP, 1)
            lane = lax.broadcasted_iota(jnp.int32, more.shape, 1)
            line = lax.broadcasted_iota(jnp.int32, more.shape, 0)
            target = jnp.where(line % (2 * each) < each, target_ref[0], target_ref[1])
            chosen = (routes == target.astype(F32)) & (lane < TOP)
            share = jnp.sum(jnp.where(chosen, more, 0.0), axis=1, keepdims=True)
            out_ref[...] = (result * share).astype(out_ref.dtype)

    first = half * (count // step)
    return pl.pallas_call(
        body,
        name="experts",
        out_shape=[
            jax.ShapeDtypeStruct((count, feat), F32),
            jax.ShapeDtypeStruct((count, feat), BF),
        ],
        grid=(count // step,),
        in_specs=[
            pl.BlockSpec(memory_space=pltpu.SMEM),
            pl.BlockSpec((step, width), lambda i: (first + i, 0)),
            pl.BlockSpec((step, width), lambda i: (first + i, 0)),
            pl.BlockSpec(w_in.shape, lambda i: (0, 0)),
            pl.BlockSpec(w_out.shape, lambda i: (0, 0)),
        ],
        out_specs=[pl.BlockSpec((step, feat), lambda i: (i, 0))] * 2,
        compiler_params=pltpu.CompilerParams(vmem_limit_bytes=48 * 1024 * 1024),
        cost_estimate=pl.CostEstimate(flops=0, bytes_accessed=0, transcendentals=0),
    )(targets, here, there, w_in, w_out)


def a2a(x):
    return lax.all_to_all(x, "ep", split_axis=0, concat_axis=0, tiled=True)


def tiles(piece, pieces, unit, inner, columns):
    per_column = inner // unit
    for j in range(2 * inner // LANES):
        u = j * pieces + piece
        row = pl.multiple_of((u % per_column) * unit, unit)
        column = pl.multiple_of((u // per_column) * LANES, LANES)
        yield row, column, j * LANES


def pack(w_in, w_out, gi, part_rows, pieces):
    inner = w_out.shape[0]
    cut = part_rows // pieces
    unit = cut // 2
    step = 4

    def body(_, gate_ref, down_ref, out_ref):
        at = pl.program_id(0) * step
        for i in range(step):
            out_ref[i, :cut, :] = gate_ref[i * cut : (i + 1) * cut, :]
            for row, column, to in tiles(at + i, pieces, unit, inner, part_rows):
                out_ref[i, cut:, to : to + LANES] = down_ref[pl.ds(row, unit), pl.ds(column, LANES)]

    return pl.pallas_call(
        body,
        name="pack",
        out_shape=jax.ShapeDtypeStruct((pieces, cut + unit, 2 * inner), BF),
        grid_spec=pltpu.PrefetchScalarGridSpec(
            num_scalar_prefetch=1,
            grid=(pieces // step,),
            in_specs=[
                pl.BlockSpec((step * cut, 2 * inner), lambda p, g: (g[0] * (pieces // step) + p, 0)),
                pl.BlockSpec((inner, part_rows), lambda p, g: (0, g[0])),
            ],
            out_specs=pl.BlockSpec((step, cut + unit, 2 * inner), lambda p, g: (p, 0, 0)),
        ),
        compiler_params=pltpu.CompilerParams(vmem_limit_bytes=32 * 1024 * 1024),
        cost_estimate=pl.CostEstimate(
            flops=0, bytes_accessed=12 * part_rows * inner, transcendentals=0
        ),
    )(gi.reshape(1), w_in, w_out)


def unpack(packed, part_rows, inner):
    pieces = packed.shape[0]
    cut = part_rows // pieces
    unit = cut // 2
    step = 4

    def body(in_ref, gate_ref, down_ref):
        at = pl.program_id(0) * step
        for i in range(step):
            gate_ref[i * cut : (i + 1) * cut, :] = in_ref[i, :cut, :]
            for row, column, to in tiles(at + i, pieces, unit, inner, part_rows):
                down_ref[pl.ds(row, unit), pl.ds(column, LANES)] = in_ref[i, cut:, to : to + LANES]

    return pl.pallas_call(
        body,
        name="unpack",
        out_shape=[
            jax.ShapeDtypeStruct((part_rows, 2 * inner), BF),
            jax.ShapeDtypeStruct((inner, part_rows), BF),
        ],
        grid=(pieces // step,),
        in_specs=[pl.BlockSpec((step, cut + unit, 2 * inner), lambda p: (p, 0, 0))],
        out_specs=[
            pl.BlockSpec((step * cut, 2 * inner), lambda p: (p, 0)),
            pl.BlockSpec((inner, part_rows), lambda p: (0, 0)),
        ],
        compiler_params=pltpu.CompilerParams(vmem_limit_bytes=32 * 1024 * 1024),
        cost_estimate=pl.CostEstimate(
            flops=0, bytes_accessed=12 * part_rows * inner, transcendentals=0
        ),
    )(packed)


def local(
    tokens_one,
    routes_one,
    gates_one,
    tokens_two,
    routes_two,
    gates_two,
    old_table,
    new_table,
    gate_up,
    down_proj,
    norm_gain,
    kv_weight,
):
    w_in = gate_up[0]
    w_out = down_proj[0]
    ep = lax.axis_size("ep")
    grp = lax.axis_size("grp")
    me = lax.axis_index("ep")
    gi = lax.axis_index("grp")
    rows = tokens_one.shape[0]
    feat = w_in.shape[0]
    inner = w_out.shape[0]
    numbers = jnp.arange(ep, dtype=jnp.int32)
    sources_new = jnp.sum(
        (new_table[:, None] == old_table[None, :]).astype(jnp.int32) * numbers[None, :], axis=1
    )
    new_here = jnp.sum((sources_new == me).astype(jnp.int32) * numbers)

    mine = join(
        [(tokens_one, gates_one.T, routes_one.T), (tokens_two, gates_two.T, routes_two.T)]
    )
    far = [4 * i for i in range(1, ep // 4)]
    blocks = [mine] + [swap(mine, "ep", d) for d in far]

    part_rows = feat // grp
    cut = part_rows // ep
    line = jnp.concatenate(blocks, axis=0)
    line, gi = lax.optimization_barrier((line, gi))
    packing = cut % 32 == 0 and inner % (cut // 2) == 0 and part_rows % LANES == 0 == inner % 64
    if packing:
        pieces = [pack(w_in, w_out, gi, part_rows, ep)]
    else:
        half_in = lax.dynamic_slice_in_dim(w_in, gi * part_rows, part_rows, 0)
        half_out = lax.dynamic_slice_in_dim(w_out, gi * part_rows, part_rows, 1)
        pieces = [half_in.reshape(ep, cut, 2 * inner), half_out.reshape(ep, inner // ep, part_rows)]
    spread = [a2a(x) for x in pieces]

    kv_blocks = [lax.optimization_barrier((kv_weight, line))[0]]
    for bit in range(grp.bit_length() - 1):
        kv_blocks = kv_blocks + [swap(x, "grp", 1 << bit) for x in kv_blocks]

    here = jnp.concatenate([line, swap(line, "ep", 2)], axis=0)
    there = swap(here, "ep", 1)
    targets = jnp.stack([me, new_here])

    kept, given = experts(here, there, 1, rows, targets, w_in, w_out)
    sent = (kept + swap(given, "ep", 1).astype(F32)).astype(BF)
    sent, here, wanted = lax.optimization_barrier((sent, here, sources_new))
    came = swap(sent, "ep", 2)
    kept, given = experts(here, there, 0, rows, targets, w_in, w_out)
    kept = kept + swap(given, "ep", 1).astype(F32) + came.astype(F32)
    kept, wanted = lax.optimization_barrier((kept, wanted))
    block = 2 * rows
    sent = [kept[(i + 1) * block : (i + 2) * block].astype(BF) for i in range(len(far))]
    came = [swap(x, "ep", d) for x, d in zip(sent, far)]
    grouped = [x[wanted] for x in spread]
    came, grouped = lax.optimization_barrier((came, grouped))
    moved = [a2a(x) for x in grouped]
    mix = kept[:block] + sum(x.astype(F32) for x in came)
    own = jnp.concatenate([tokens_one, tokens_two], axis=0)
    hidden_all = (own.astype(F32) + mix).astype(BF)

    if packing:
        gate_up_new, down_proj_new = unpack(moved[0], part_rows, inner)
    else:
        gate_up_new = moved[0].reshape(part_rows, 2 * inner)
        down_proj_new = moved[1].reshape(inner, part_rows)

    normed = rms_norm(hidden_all, norm_gain)
    blocks = [jnp.dot(normed, w, preferred_element_type=F32).astype(BF) for w in kv_blocks]
    kv = jnp.take(jnp.stack(blocks), gi ^ jnp.arange(grp), axis=0)
    kv = kv.transpose(1, 0, 2).reshape(2 * rows, -1)
    return (
        hidden_all[:rows],
        kv[:rows],
        hidden_all[rows:],
        kv[rows:],
        gate_up_new[None],
        down_proj_new[None],
    )


def solution(mesh):
    tok = P(("grp", "ep"), None)
    return jax.shard_map(
        local,
        mesh=mesh,
        in_specs=(
            tok,
            tok,
            tok,
            tok,
            tok,
            tok,
            P(),
            P(),
            P("ep", None, None),
            P("ep", None, None),
            P(),
            P(None, "grp"),
        ),
        out_specs=(tok, tok, tok, tok, P("ep", "grp", None), P("ep", None, "grp")),
        check_vma=False,
    )
```
